256 devices in a mesh: space: 64 (over x, z, core), rep: 4 (over y).
Axes of the slice: x: 4, y: 4, z: 8, core: 2. Of those that a mesh axis runs over, the one named last changes fastest.
Arguments:
- voxel_feats: bfloat16 [4, 96, 98304], P('rep', None, 'space'), may hold values from -6 to 6
- kernel_map: int32 [4, 27, 98304], P('rep', None, 'space'), may hold values from 0 to 2304, as said below
- halo_down: int32 [4, 24576], P('rep', 'space'), may hold values from 0 to 1535
- halo_up: int32 [4, 24576], P('rep', 'space'), may hold values from 0 to 1535
- route_slot: int32 [4, 98304], P('rep', 'space'), may hold values from 0 to 1535, as said below
- recv_target: int32 [4, 98304], P('rep', 'space'), may hold values from 0 to 6143, as said below
- subm_weight: bfloat16 [27, 96, 96], replicated, may hold values from -0.125 to 0.125
- down_weight: bfloat16 [8, 96, 192], replicated, may hold values from -0.21875 to 0.21875
- coarse_grad: bfloat16 [4, 192, 49152], P('rep', None, 'space'), may hold values from -0.0134887695 to 0.0134887695
Outputs:
- coarse_feats: bfloat16 [4, 192, 49152], P('rep', None, 'space')
- subm_grad: float32 [27, 96, 96], replicated
- down_grad: float32 [8, 96, 192], replicated
The draws below stay inside these ranges and needn't reach their ends.
Inputs may be any that keep to these rules, and one draw needn't show every extreme that they name: `kernel_map`: row 27 // 2 (the centre) of a device's block names the voxel itself. Other entries: below 1536 a voxel of the same device; 1536 to 1919 the rows received from the lower neighbour in space, in the order of its halo_up list; the next 384 those from the upper neighbour in the order of its halo_down list; 2304 an absent neighbour. `route_slot`: distinct within a device's block: each device sends exactly 24 rows to every new owner, so every slot is used. `recv_target`: distinct within a device's block; entry s * 24 + j belongs to the row that slot j of device s brings.
All inputs are finite; a program needn't handle non-finite values.
Results may differ from the reference program's by a relative error of at most 0.0053.
Values may be sent and summed in bfloat16 or wider, within the bound.
A program may use at most 128 MiB of HBM per device.

```python
from functools import partial
import jax
import jax.numpy as jnp

C = 96
C2 = 192
OFFSETS = 27
CHILDREN = 8
VOX = 1536
HALO = 384
COARSE = 768
CAP = 24
N_SPACE = 64
N_REP = 4


def draw_kernel_map(key, part):
    key = jax.random.fold_in(key, 5)
    kind_key, own_key, rim_key = jax.random.split(key, 3)
    shape = (N_REP, OFFSETS, N_SPACE * VOX)
    kinds = jax.random.randint(kind_key, shape, 0, 8)
    own_rows = jax.random.randint(own_key, shape, 0, VOX)
    rim_rows = jax.random.randint(rim_key, shape, 0, HALO)
    absent = VOX + 2 * HALO
    chosen = jnp.where(kinds < 3, absent, jnp.where(kinds < 6, own_rows, jnp.where(kinds == 6, VOX + rim_rows, VOX + HALO + rim_rows)))
    centre = (jnp.arange(N_SPACE * VOX) % VOX)[None, None, :]
    offset_ids = jnp.arange(OFFSETS)[None, :, None]
    return jnp.where(offset_ids == OFFSETS // 2, centre, chosen).astype(jnp.int32)


def sender_perm(sender_key):
    return jax.random.permutation(sender_key, N_SPACE * CAP)


def draw_route_slot(key, part):
    key = jax.random.fold_in(key, 11)
    perms = jax.vmap(sender_perm)(jax.random.split(key, N_REP * N_SPACE))
    return perms.reshape(N_REP, N_SPACE * VOX).astype(jnp.int32)


def receiver_cells(receiver_key):
    return jax.random.permutation(receiver_key, CHILDREN * COARSE)[:N_SPACE * CAP]


def draw_recv_target(key, part):
    key = jax.random.fold_in(key, 9)
    picked = jax.vmap(receiver_cells)(jax.random.split(key, N_REP * N_SPACE))
    return picked.reshape(N_REP, N_SPACE * N_SPACE * CAP).astype(jnp.int32)


def with_ends(drawn, stream_key, smallest, largest):
    longest = drawn.shape.index(max(drawn.shape))
    spots = []
    for shift in (0, 1):
        where = [jax.random.randint(jax.random.fold_in(stream_key, axis), (), 0, length) for axis, length in enumerate(drawn.shape)]
        where[longest] = (where[longest] + shift) % drawn.shape[longest]
        spots.append(tuple(where))
    return drawn.at[spots[0]].set(smallest).at[spots[1]].set(largest)


def block_levels(key, dims, pieces, low, high):
    def one(position, shards_of):
        heights = jax.random.uniform(jax.random.fold_in(jax.random.fold_in(key, 6), position), (shards_of,), jnp.float32, low / len(pieces), high / len(pieces))
        return jnp.repeat(jnp.exp(heights), dims[position] // shards_of).reshape((-1,) + (1,) * (len(dims) - position - 1))

    level = one(*pieces[0])
    for cut in pieces[1:]:
        level = level * one(*cut)
    return level


def noise(key, extent, scale, reach, cuts=(), kind=jnp.bfloat16):
    gain = block_levels(key, extent, cuts, -0.22, 0.18) if cuts else 1.0
    array = jax.random.normal(key, extent, jnp.float32) * scale * gain
    return jnp.minimum(jnp.maximum(array, -reach), reach).astype(kind)


def setup_inputs(seed: int = 0) -> dict:
    key_of = jax.random.split(jax.random.key(seed), 10)
    return {
        "voxel_feats": noise(key_of[0], (N_REP, C, N_SPACE * VOX), 1.0, 6.0, ((0, 4), (2, 64))),
        "kernel_map": draw_kernel_map(jax.random.fold_in(key_of[9], 71), 0),
        "halo_down": with_ends(jax.random.randint(key_of[2], (N_REP, N_SPACE * HALO), 0, VOX), jax.random.fold_in(key_of[2], 1), 0, VOX - 1).astype(jnp.int32),
        "halo_up": with_ends(jax.random.randint(key_of[3], (N_REP, N_SPACE * HALO), 0, VOX), jax.random.fold_in(key_of[3], 1), 0, VOX - 1).astype(jnp.int32),
        "route_slot": draw_route_slot(jax.random.fold_in(key_of[9], 71), 0),
        "recv_target": draw_recv_target(jax.random.fold_in(key_of[9], 71), 0),
        "subm_weight": noise(key_of[6], (OFFSETS, C, C), (OFFSETS * C) ** -0.5, 0.125),
        "down_weight": noise(key_of[7], (CHILDREN, C, C2), (CHILDREN * C) ** -0.5, 0.21875),
        "coarse_grad": noise(key_of[8], (N_REP, C2, N_SPACE * COARSE), ((N_REP * N_SPACE * COARSE) ** -0.5), 0.0134887695, ((0, 4), (2, 64))),
    }


def take_columns(matrix, columns):
    return jnp.take(matrix, columns, axis=1)


def place_columns(width, values, columns):
    return jnp.zeros((values.shape[0], width), values.dtype).at[:, columns].set(values)


def swap_blocks(blocks):
    return blocks.reshape(N_SPACE, blocks.shape[1], N_SPACE, CAP).transpose(2, 1, 0, 3).reshape(N_SPACE, blocks.shape[1], N_SPACE * CAP)


def reference(voxel_feats, kernel_map, halo_down, halo_up, route_slot, recv_target, subm_weight, down_weight, coarse_grad):
    subm_total = jnp.zeros((OFFSETS, C, C), jnp.float32)
    down_total = jnp.zeros((CHILDREN, C, C2), jnp.float32)
    coarse_parts = []
    for replica in range(N_REP):
        fine_in = voxel_feats[replica].reshape(C, N_SPACE, VOX).transpose(1, 0, 2)
        maps = kernel_map[replica].reshape(OFFSETS, N_SPACE, VOX).transpose(1, 0, 2)
        lists_up = halo_up[replica].reshape(N_SPACE, HALO)
        lists_down = halo_down[replica].reshape(N_SPACE, HALO)
        sent_up = jax.vmap(take_columns)(fine_in, lists_up)
        sent_down = jax.vmap(take_columns)(fine_in, lists_down)
        edge = jnp.zeros((1, C, HALO), jnp.bfloat16)
        from_lower = jnp.concatenate([edge, sent_up[:-1]], axis=0)
        from_upper = jnp.concatenate([sent_down[1:], edge], axis=0)
        stacked = jnp.concatenate([fine_in, from_lower, from_upper, jnp.zeros((N_SPACE, C, 1), jnp.bfloat16)], axis=2)
        conv_sum = jnp.zeros((N_SPACE, C, VOX), jnp.float32)
        for offset in range(OFFSETS):
            gathered = jax.vmap(take_columns)(stacked, maps[:, offset])
            conv_sum = conv_sum + jnp.einsum("io,div->dov", subm_weight[offset].astype(jnp.float32), gathered.astype(jnp.float32))
        pre_act = fine_in.astype(jnp.float32) + conv_sum
        sigmoid_act = jax.nn.sigmoid(pre_act)
        fine_out = (pre_act * sigmoid_act).astype(jnp.bfloat16)
        slots = N_SPACE * CAP
        routes = route_slot[replica].reshape(N_SPACE, VOX)
        targets = recv_target[replica].reshape(N_SPACE, slots)
        sent = jax.vmap(partial(place_columns, slots))(fine_out, routes)
        received = swap_blocks(sent)
        cells = jax.vmap(partial(place_columns, CHILDREN * COARSE))(received, targets)
        cells = cells.reshape(N_SPACE, C, CHILDREN, COARSE)
        coarse = jnp.einsum("kio,dikc->doc", down_weight.astype(jnp.float32), cells.astype(jnp.float32)).astype(jnp.bfloat16)
        coarse_parts.append(coarse.transpose(1, 0, 2).reshape(C2, N_SPACE * COARSE))
        cotangent = coarse_grad[replica].reshape(C2, N_SPACE, COARSE).transpose(1, 0, 2)
        cell_grad = jnp.einsum("kio,doc->dikc", down_weight.astype(jnp.float32), cotangent.astype(jnp.float32)).astype(jnp.bfloat16)
        cell_grad = cell_grad.reshape(N_SPACE, C, CHILDREN * COARSE)
        down_total = down_total + jnp.einsum("dikc,doc->kio", cells.astype(jnp.float32), cotangent.astype(jnp.float32))
        back = jax.vmap(take_columns)(cell_grad, targets)
        returned = swap_blocks(back)
        fine_grad = jax.vmap(take_columns)(returned, routes)
        pre_grad = (fine_grad.astype(jnp.float32) * sigmoid_act * (1.0 + pre_act * (1.0 - sigmoid_act))).astype(jnp.bfloat16)
        for offset in range(OFFSETS):
            gathered = jax.vmap(take_columns)(stacked, maps[:, offset])
            term = jnp.einsum("div,dov->io", gathered.astype(jnp.float32), pre_grad.astype(jnp.float32))
            subm_total = subm_total.at[offset].add(term)
    return jnp.stack(coarse_parts), subm_total, down_total
```

```python
import functools

import jax
import jax.numpy as jnp
from jax import lax
from jax.experimental import pallas as pl
from jax.experimental.pallas import tpu as pltpu
from jax.sharding import PartitionSpec as P

C = 96
C2 = 192
OFFSETS = 27
CHILDREN = 8
VOX = 1536
HALO = 384
COARSE = 768
CAP = 24
N_SPACE = 64
N_REP = 4
L = 128
HALF = (VOX + 2 * HALO) // 2
CHUNK = 256
MIB = 2**20
MESH = pl.DeviceIdType.MESH
BF = jnp.bfloat16
F32 = jnp.float32

SUBM_ROWS = OFFSETS * C
DOWN_ROWS = CHILDREN * C
ROWS = 4096
PIECE = ROWS // 32
PART = PIECE // 8


def lane_iota(rows):
    return lax.broadcasted_iota(jnp.int32, (rows, L), 1).astype(F32).astype(BF)


def split_index(index):
    top = jnp.floor(index * (1.0 / L))
    return top.astype(BF), (index - L * top).astype(BF)


def onehot(top, low, iota, tiles):
    rows = iota.shape[0]
    zero = jnp.zeros((), BF)
    hit = jnp.where(jnp.broadcast_to(low, (rows, L)) == iota, jnp.ones((), BF), zero)
    tops = jnp.broadcast_to(top, (rows, L))
    return jnp.concatenate(
        [jnp.where(tops == jnp.asarray(t, BF), hit, zero) for t in range(tiles)], axis=1
    )


def onehot_of_row(row, rows):
    spread = jnp.broadcast_to(row, (rows, row.shape[1])).astype(BF)
    iota = lax.broadcasted_iota(jnp.int32, spread.shape, 0).astype(F32).astype(BF)
    return jnp.where(spread == iota, jnp.ones((), BF), jnp.zeros((), BF))


def padded_rows(x, rows):
    return jnp.concatenate([x, jnp.zeros((rows - x.shape[0], x.shape[1]), x.dtype)], axis=0)


def dot(a, b):
    return jnp.dot(a, b, preferred_element_type=F32)


def conv_kernel(
    feats_ref, kmap_ref, up_ref, down_ref, route_ref, ret_ref, w_ref,
    sent_ref, sgrad_ref,
    own, table, rettab, wpad, index, gath, fine, acc, hsend, hrecv, send_sem, recv_sem,
):
    me, rep = lax.axis_index("space"), lax.axis_index("rep")
    above, below = (me + 1) % N_SPACE, (me + N_SPACE - 1) % N_SPACE
    barrier = pltpu.get_barrier_semaphore()
    for peer in (above, below):
        pl.semaphore_signal(barrier, inc=1, device_id=(peer, rep), device_id_type=MESH)
    own[...] = padded_rows(feats_ref[...].astype(F32), L).T.astype(BF)
    halo_rows = jnp.concatenate([up_ref[...], down_ref[...]], axis=1).astype(F32)
    halo_cols = jnp.broadcast_to(halo_rows, (8, 2 * HALO)).T
    iota_h = lane_iota(HALO)
    for side in range(2):
        top, low = split_index(halo_cols[side * HALO:(side + 1) * HALO, :1])
        hsend[side] = dot(onehot(top, low, iota_h, VOX // L), own[...]).astype(BF)

    def halo_copy(side, peer):
        return pltpu.make_async_remote_copy(
            src_ref=hsend.at[side], dst_ref=hrecv.at[side],
            send_sem=send_sem.at[side], recv_sem=recv_sem.at[side],
            device_id=(peer, rep), device_id_type=MESH,
        )

    to_upper, to_lower = halo_copy(0, above), halo_copy(1, below)
    pl.semaphore_wait(barrier, 2)
    to_upper.start()
    to_lower.start()
    wpad[...] = jnp.zeros_like(wpad)
    for k in range(OFFSETS):
        wpad[k * L:k * L + C, :C] = w_ref[k]
    rows = jnp.concatenate([kmap_ref[...], route_ref[...]], axis=0).astype(F32)
    index[...] = padded_rows(rows, L).T
    ret = padded_rows(ret_ref[...].astype(F32), L).T.astype(BF)
    rettab[:, :L] = ret[:VOX // 2]
    rettab[:, L:] = ret[VOX // 2:]
    acc[...] = jnp.zeros_like(acc)
    table[:, :L] = own[:HALF]
    table[:VOX - HALF, L:] = own[HALF:]

    to_upper.wait()
    to_lower.wait()
    lower = jnp.where(me > 0, hrecv[0], jnp.zeros((), BF))
    upper = jnp.where(me < N_SPACE - 1, hrecv[1], jnp.zeros((), BF))
    table[VOX - HALF:VOX - HALF + HALO, L:] = lower
    table[VOX - HALF + HALO:, L:] = upper
    iota_c = lane_iota(CHUNK)

    @pl.loop(0, VOX // CHUNK)
    def _(step):
        here = pl.ds(pl.multiple_of(step * CHUNK, CHUNK), CHUNK)
        which = index[here, :]
        second = jnp.where(which >= HALF, 1.0, 0.0)
        top, low = split_index(which - HALF * second)
        for k in range(OFFSETS):
            both = dot(onehot(top[:, k:k + 1], low[:, k:k + 1], iota_c, HALF // L), table[...])
            picked = jnp.where(second[:, k:k + 1] > 0.5, both[:, L:], both[:, :L])
            gath[:, k * L:(k + 1) * L] = picked.astype(BF)
        pre = own[here, :].astype(F32) + dot(gath[...], wpad[...])
        sig = jax.nn.sigmoid(pre)
        fine[here, :] = (pre * sig).astype(BF)
        slot = which[:, OFFSETS:OFFSETS + 1]
        far = jnp.where(slot >= VOX // 2, 1.0, 0.0)
        top, low = split_index(slot - (VOX // 2) * far)
        both = dot(onehot(top, low, iota_c, VOX // 2 // L), rettab[...])
        fine_grad = jnp.where(far > 0.5, both[:, L:], both[:, :L])
        pre_grad = fine_grad * sig * (1.0 + pre * (1.0 - sig))
        acc[...] += dot(pre_grad.T.astype(BF), gath[...])

    route = route_ref[...].astype(F32)
    for block in range(VOX // CHUNK):
        hits = onehot_of_row(route - block * CHUNK, CHUNK)
        sent = dot(hits, fine[...]).T
        sent_ref[:, block * CHUNK:(block + 1) * CHUNK] = sent[:C].astype(BF)
    for k in range(OFFSETS):
        sgrad_ref[k * C:(k + 1) * C, :] = acc[:, k * L:(k + 1) * L].T[:C]


def conv_call(feats, kmap, up, down, route, ret, w):
    vmem = pl.BlockSpec(memory_space=pltpu.VMEM)
    return pl.pallas_call(
        conv_kernel,
        out_shape=(
            jax.ShapeDtypeStruct((C, VOX), BF),
            jax.ShapeDtypeStruct((SUBM_ROWS, L), F32),
        ),
        in_specs=[vmem] * 7,
        out_specs=(vmem, vmem),
        scratch_shapes=[
            pltpu.VMEM((VOX, L), BF),
            pltpu.VMEM((HALF, 2 * L), BF),
            pltpu.VMEM((VOX // 2, 2 * L), BF),
            pltpu.VMEM((OFFSETS * L, L), BF),
            pltpu.VMEM((VOX, L), F32),
            pltpu.VMEM((CHUNK, OFFSETS * L), BF),
            pltpu.VMEM((VOX, L), BF),
            pltpu.VMEM((L, OFFSETS * L), F32),
            pltpu.VMEM((2, HALO, L), BF),
            pltpu.VMEM((2, HALO, L), BF),
            pltpu.SemaphoreType.DMA((2,)),
            pltpu.SemaphoreType.DMA((2,)),
        ],
        compiler_params=pltpu.CompilerParams(
            collective_id=0, has_side_effects=True, vmem_limit_bytes=48 * MIB
        ),
        name="conv",
    )(feats, kmap, up, down, route, ret, w)


def reduce_kernel(
    subm_ref, down_ref, sgrad_ref, dgrad_ref,
    mine, pair, plane, spread, column, line, full, psend, zsend,
    core_sems, plane_sems, z_sems, zback_sems, back_sems, coreback_sems,
):
    space, y = lax.axis_index("space"), lax.axis_index("rep")
    core, z, x = space % 2, (space // 2) % 8, space // 16
    at = lambda xx, zz, cc: (xx * 8 + zz) * 2 + cc
    partner = (at(x, z, 1 - core), y)
    plane_peers = [(at((x + d // 4) % 4, z, core), (y + d % 4) % 4) for d in range(16)]
    plane_index = [((x + d // 4) % 4) * 4 + (y + d % 4) % 4 for d in range(16)]
    plane_from = [((x + 4 - d // 4) % 4) * 4 + (y + 4 - d % 4) % 4 for d in range(16)]
    z_peers = [(at(x, (z + d) % 8, core), y) for d in range(8)]
    z_index = [(z + d) % 8 for d in range(8)]
    z_from = [(z + 8 - d) % 8 for d in range(8)]
    barrier = pltpu.get_barrier_semaphore()
    peers = [partner] + plane_peers[1:] + z_peers[1:]
    for peer in peers:
        pl.semaphore_signal(barrier, inc=1, device_id=peer, device_id_type=MESH)

    def remote(src, dst, sems, i, peer):
        return pltpu.make_async_remote_copy(
            src_ref=src, dst_ref=dst, send_sem=sems.at[0, i], recv_sem=sems.at[1, i],
            device_id=peer, device_id_type=MESH,
        )

    def rows(i, n):
        return pl.ds(pl.multiple_of(i * n, n), n)

    mine[:SUBM_ROWS] = subm_ref[...].astype(BF)
    mine[SUBM_ROWS:SUBM_ROWS + DOWN_ROWS] = down_ref[:, :L].astype(BF)
    tail = SUBM_ROWS + DOWN_ROWS
    mine[tail:tail + DOWN_ROWS // 2] = jnp.concatenate(
        [down_ref[:DOWN_ROWS // 2, L:], down_ref[DOWN_ROWS // 2:, L:]], axis=1
    ).astype(BF)
    mine[tail + DOWN_ROWS // 2:] = jnp.zeros((ROWS - tail - DOWN_ROWS // 2, L), BF)
    pl.semaphore_wait(barrier, len(peers))

    to_partner = []
    for d in range(16):
        p = plane_index[d]
        copy = remote(mine.at[rows((1 - core) * 16 + p, PIECE)], pair.at[rows(p, PIECE)], core_sems, d, partner)
        copy.start()
        to_partner.append(copy)
    to_plane = []
    for d in list(range(1, 16)) + [0]:
        p = plane_index[d]
        to_partner[d].wait_recv()
        both = mine[rows(core * 16 + p, PIECE)].astype(F32) + pair[rows(p, PIECE)].astype(F32)
        if d == 0:
            total = both
        else:
            psend[d] = both.astype(BF)
            copy = remote(psend.at[d], plane.at[d], plane_sems, d, plane_peers[d])
            copy.start()
            to_plane.append(copy)
    for d in range(1, 16):
        to_plane[d - 1].wait_recv()
        total += plane[d].astype(F32)
    zsend[...] = total.astype(BF)
    line[...] = total
    to_z = []
    for d in range(1, 8):
        copy = remote(zsend.at[rows(z_index[d], PART)], column.at[d], z_sems, d, z_peers[d])
        copy.start()
        to_z.append(copy)
    part = line[rows(z, PART)]
    for d in range(1, 8):
        to_z[d - 1].wait_recv()
        part += column[d].astype(F32)
    spread[rows(z, PART)] = part.astype(BF)
    for d in range(1, 8):
        to_z[d - 1].wait_send()
    back_z = []
    for d in range(1, 8):
        copy = remote(spread.at[rows(z, PART)], spread.at[rows(z, PART)], zback_sems, d, z_peers[d])
        copy.start()
        back_z.append(copy)
    for d in range(1, 8):
        back_z[d - 1].wait_recv()
    here = core * 16 + plane_index[0]
    full[rows(here, PIECE)] = spread[...]
    back = []
    for d in range(1, 16):
        copy = remote(spread, full.at[rows(here, PIECE)], back_sems, d, plane_peers[d])
        copy.start()
        back.append(copy)
    over = []
    for d in range(16):
        if d:
            back[d - 1].wait_recv()
        where = rows(core * 16 + plane_from[d], PIECE)
        copy = remote(full.at[where], full.at[where], coreback_sems, d, partner)
        copy.start()
        over.append(copy)
    for copy in over:
        copy.wait_recv()
    for k in range(OFFSETS):
        sgrad_ref[k] = full[k * C:(k + 1) * C, :C].astype(F32)
    for k in range(CHILDREN):
        dgrad_ref[k, :, :L] = full[SUBM_ROWS + k * C:SUBM_ROWS + (k + 1) * C].astype(F32)
        half, q = divmod(k, CHILDREN // 2)
        dgrad_ref[k, :, L:] = full[tail + q * C:tail + (q + 1) * C, half * 64:half * 64 + 64].astype(F32)
    for copy in to_partner + to_plane + back_z + back + over:
        copy.wait_send()


def reduce_call(subm, down):
    vmem = pl.BlockSpec(memory_space=pltpu.VMEM)
    return pl.pallas_call(
        reduce_kernel,
        out_shape=(
            jax.ShapeDtypeStruct((OFFSETS, C, C), F32),
            jax.ShapeDtypeStruct((CHILDREN, C, C2), F32),
        ),
        in_specs=[vmem] * 2,
        out_specs=(vmem, vmem),
        scratch_shapes=[
            pltpu.VMEM((ROWS, L), BF),
            pltpu.VMEM((ROWS // 2, L), BF),
            pltpu.VMEM((16, PIECE, L), BF),
            pltpu.VMEM((PIECE, L), BF),
            pltpu.VMEM((8, PART, L), BF),
            pltpu.VMEM((PIECE, L), F32),
            pltpu.VMEM((ROWS, L), BF),
            pltpu.VMEM((16, PIECE, L), BF),
            pltpu.VMEM((PIECE, L), BF),
            pltpu.SemaphoreType.DMA((2, 16)),
            pltpu.SemaphoreType.DMA((2, 16)),
            pltpu.SemaphoreType.DMA((2, 8)),
            pltpu.SemaphoreType.DMA((2, 8)),
            pltpu.SemaphoreType.DMA((2, 16)),
            pltpu.SemaphoreType.DMA((2, 16)),
        ],
        compiler_params=pltpu.CompilerParams(
            collective_id=1, has_side_effects=True, vmem_limit_bytes=48 * MIB
        ),
        name="reduce",
    )(subm, down)


def per_device(
    voxel_feats, kernel_map, halo_down, halo_up, route_slot, recv_target,
    subm_weight, down_weight, coarse_grad,
):
    feats = voxel_feats[0]
    cotangent = coarse_grad[0]
    cell_grad = jnp.einsum("kio,oc->ikc", down_weight, cotangent, preferred_element_type=F32).astype(BF)
    cell_grad = cell_grad.reshape(C, CHILDREN * COARSE)
    outbound = jnp.take(cell_grad, recv_target[0], axis=1)
    returned = lax.all_to_all(outbound, "space", split_axis=1, concat_axis=1, tiled=True)
    outgoing, subm_local = conv_call(
        feats, kernel_map[0], halo_up, halo_down, route_slot, returned, subm_weight
    )
    received = lax.all_to_all(outgoing, "space", split_axis=1, concat_axis=1, tiled=True)
    cells = jnp.zeros((C, CHILDREN * COARSE), BF).at[:, recv_target[0]].set(received)
    cells = cells.reshape(C, CHILDREN, COARSE)
    coarse = jnp.einsum("kio,ikc->oc", down_weight, cells, preferred_element_type=F32).astype(BF)
    down_local = jnp.einsum("ikc,oc->kio", cells, cotangent, preferred_element_type=F32)
    subm_total, down_total = reduce_call(subm_local, down_local.reshape(DOWN_ROWS, C2))
    return (coarse[None], subm_total, down_total)


def solution(mesh):
    in_specs = (
        P("rep", None, "space"),
        P("rep", None, "space"),
        P("rep", "space"),
        P("rep", "space"),
        P("rep", "space"),
        P("rep", "space"),
        P(),
        P(),
        P("rep", None, "space"),
    )
    out_specs = (P("rep", None, "space"), P(), P())
    return jax.shard_map(
        per_device, mesh=mesh, in_specs=in_specs, out_specs=out_specs, check_vma=False
    )
```

```python
import jax
import jax.numpy as jnp
from jax import lax
from jax.experimental import pallas as pl
from jax.experimental.pallas import tpu as pltpu
from jax.sharding import PartitionSpec as P

C = 96
C2 = 192
OFFSETS = 27
CHILDREN = 8
VOX = 1536
HALO = 384
COARSE = 768
CAP = 24
N_SPACE = 64
N_REP = 4
L = 128
PAD = 32
HALF = (VOX + 2 * HALO) // 2
CHUNK = 256
PEERS_AT_ONCE = 8
MIB = 2**20
MESH = pl.DeviceIdType.MESH
BF = jnp.bfloat16
F32 = jnp.float32

SUBM_TILES = 21
DOWN_TILES = 6
SUBM_SHARE = 64
DOWN_SHARE = 48


def lane_iota(rows):
    return lax.broadcasted_iota(jnp.int32, (rows, L), 1).astype(F32).astype(BF)


def split_index(index):
    top = jnp.floor(index * (1.0 / L))
    return top.astype(BF), (index - L * top).astype(BF)


def onehot(top, low, iota, tiles):
    rows = iota.shape[0]
    zero = jnp.zeros((), BF)
    hit = jnp.where(jnp.broadcast_to(low, (rows, L)) == iota, jnp.ones((), BF), zero)
    tops = jnp.broadcast_to(top, (rows, L))
    return jnp.concatenate(
        [jnp.where(tops == jnp.asarray(t, BF), hit, zero) for t in range(tiles)], axis=1
    )


def onehot_of_row(row, rows):
    spread = jnp.broadcast_to(row, (rows, row.shape[1])).astype(BF)
    iota = lax.broadcasted_iota(jnp.int32, spread.shape, 0).astype(F32).astype(BF)
    return jnp.where(spread == iota, jnp.ones((), BF), jnp.zeros((), BF))


def padded_rows(x, rows):
    return jnp.concatenate([x, jnp.zeros((rows - x.shape[0], x.shape[1]), x.dtype)], axis=0)


def dot(a, b):
    return jnp.dot(a, b, preferred_element_type=F32)


def aligned(i, n):
    return pl.ds(pl.multiple_of(i * n, n), n)


def lanes_of_tile(t):
    q, r = divmod(t, 3)
    first = 4 * q + r
    return ((first, 32 * r, C), (first + 1, 0, 32 * (r + 1)))


def tiles_of_block(k):
    q, r = divmod(k, 4)
    pieces = []
    if r:
        pieces.append((3 * q + r - 1, L - 32 * r, L))
    if r < 3:
        pieces.append((3 * q + r, 0, C - 32 * r))
    return pieces


class Place:
    def __init__(self):
        space, y = lax.axis_index("space"), lax.axis_index("rep")
        core, z, x = space % 2, (space // 2) % 8, space // 16
        at = lambda xx, zz, cc: (xx * 8 + zz) * 2 + cc
        self.space, self.rep, self.core, self.z = space, y, core, z
        self.partner = (at(x, z, 1 - core), y)
        self.plane = [(at((x + d // 4) % 4, z, core), (y + d % 4) % 4) for d in range(16)]
        self.plane_to = [((x + d // 4) % 4) * 4 + (y + d % 4) % 4 for d in range(16)]
        self.plane_from = [((x + 4 - d // 4) % 4) * 4 + (y + 4 - d % 4) % 4 for d in range(16)]
        self.column = [(at(x, (z + d) % 8, core), y) for d in range(8)]
        self.column_from = [(z + 8 - d) % 8 for d in range(8)]


def remote(src, dst, sems, i, peer):
    return pltpu.make_async_remote_copy(
        src_ref=src, dst_ref=dst, send_sem=sems.at[0, i], recv_sem=sems.at[1, i],
        device_id=peer, device_id_type=MESH,
    )


class Reducer:
    @staticmethod
    def scratch(share):
        return [
            pltpu.VMEM((32 * share, L), F32),
            pltpu.VMEM((16 * share, L), BF),
            pltpu.VMEM((16 * share, L), BF),
            pltpu.VMEM((16, share, L), BF),
            pltpu.VMEM((16, share, L), BF),
            pltpu.VMEM((share, L), BF),
            pltpu.VMEM((8, share, L), BF),
            pltpu.VMEM((32 * share, L), BF),
            pltpu.SemaphoreType.DMA((2, 16)),
            pltpu.SemaphoreType.DMA((2, 16)),
            pltpu.SemaphoreType.DMA((2, 8)),
            pltpu.SemaphoreType.DMA((2, 16)),
            pltpu.SemaphoreType.DMA((2, 16)),
        ]

    def __init__(self, place, share, refs):
        self.place, self.share = place, share
        (self.mine, self.theirs, self.pair, self.psend, self.plane, self.zsend, self.column, self.full,
         self.pair_sems, self.plane_sems, self.z_sems, self.back_sems, self.over_sems) = refs
        self.sends = []

    def go(self, copy):
        copy.start()
        self.sends.append(copy)
        return copy

    def start_pair(self):
        p, n = self.place, self.share
        self.theirs[...] = self.mine[aligned(1 - p.core, 16 * n)].astype(BF)
        self.in_pair = []
        for d in range(16):
            at = aligned(p.plane_to[d], n)
            self.in_pair.append(self.go(
                remote(self.theirs.at[at], self.pair.at[at], self.pair_sems, d, p.partner)))

    def start_plane(self):
        p, n = self.place, self.share
        self.in_plane = []
        for d in list(range(1, 16)) + [0]:
            self.in_pair[d].wait_recv()
            both = (self.mine[aligned(p.core * 16 + p.plane_to[d], n)]
                    + self.pair[aligned(p.plane_to[d], n)].astype(F32))
            if d:
                self.psend[d] = both.astype(BF)
                self.in_plane.append(self.go(
                    remote(self.psend.at[d], self.plane.at[d], self.plane_sems, d, p.plane[d])))
        self.total = both

    def start_column(self):
        p = self.place
        total = self.total
        for d in range(1, 16):
            self.in_plane[d - 1].wait_recv()
            total += self.plane[d].astype(F32)
        self.zsend[...] = total.astype(BF)
        self.in_column = []
        for d in range(1, 8):
            self.in_column.append(self.go(
                remote(self.zsend, self.column.at[p.z], self.z_sems, d, p.column[d])))
        self.column[p.z] = total.astype(BF)

    def start_back(self):
        p, n = self.place, self.share
        for copy in self.in_column:
            copy.wait_recv()
        total = self.column[0].astype(F32)
        for z in range(1, 8):
            total += self.column[z].astype(F32)
        here = aligned(p.core * 16 + p.plane_to[0], n)
        self.full[here] = total.astype(BF)
        self.in_back = []
        for d in range(1, 16):
            self.in_back.append(self.go(
                remote(self.full.at[here], self.full.at[here], self.back_sems, d, p.plane[d])))

    def start_over(self):
        p, n = self.place, self.share
        self.in_over = []
        for d in range(16):
            if d:
                self.in_back[d - 1].wait_recv()
            at = aligned(p.core * 16 + p.plane_from[d], n)
            self.in_over.append(self.go(
                remote(self.full.at[at], self.full.at[at], self.over_sems, d, p.partner)))

    def finish(self):
        for copy in self.in_over:
            copy.wait_recv()

    def drain(self):
        for copy in self.sends:
            copy.wait_send()


def pack(block, tiles, count):
    out = []
    for t in range(tiles):
        parts = []
        for k, lo, hi in lanes_of_tile(t):
            if k < count:
                parts.append(block(k, lo, hi))
            else:
                parts.append(jnp.zeros_like(block(0, 0, hi - lo)))
        out.append(jnp.concatenate(parts, axis=1))
    return out


def swap_copy(src, dst, send_sem, recv_sem, peer, me, rep):
    return pltpu.make_async_remote_copy(
        src_ref=src.at[peer], dst_ref=dst.at[me], send_sem=send_sem, recv_sem=recv_sem,
        device_id=(peer, rep), device_id_type=MESH,
    )


def wait_swapped(src, dst, send_sem, recv_sem, me, rep, sent):
    others = pl.ds(0, N_SPACE - 1)
    copies = pltpu.make_async_remote_copy(
        src_ref=src.at[others], dst_ref=dst.at[others], send_sem=send_sem, recv_sem=recv_sem,
        device_id=((me + 1) % N_SPACE, rep), device_id_type=MESH,
    )
    if sent:
        copies.wait_send()
    else:
        copies.wait_recv()


def rows_of_group(ref, group):
    return jnp.concatenate(
        [ref[group * PEERS_AT_ONCE + i].astype(F32)[:CAP] for i in range(PEERS_AT_ONCE)], axis=0
    )


def step_kernel(
    feats_ref, kmap_ref, up_ref, down_ref, route_ref, target_ref, w_ref, wd_ref, cg_ref,
    coarse_ref, sgrad_ref, dgrad_ref,
    own, table, rettab, wpad, wdpad, index, gath, pre_buf, fine, acc, cgt, back, cells_in, dacc,
    hsend, hrecv, bsend, brecv, fsend, frecv, halo_sems, swap_sems, *reduce_refs,
):
    place = Place()
    me, rep = place.space, place.rep
    above, below = (me + 1) % N_SPACE, (me + N_SPACE - 1) % N_SPACE
    barrier = pltpu.get_barrier_semaphore()

    @pl.loop(1, N_SPACE)
    def _(d):
        pl.semaphore_signal(barrier, inc=1, device_id=((me + d) % N_SPACE, rep), device_id_type=MESH)

    others = [place.plane[d] for d in range(16) if d % 4]
    for peer in others:
        pl.semaphore_signal(barrier, inc=1, device_id=peer, device_id_type=MESH)

    own[...] = padded_rows(feats_ref[0].astype(F32), L).T.astype(BF)
    halo_rows = jnp.concatenate([up_ref[...], down_ref[...]], axis=1).astype(F32)
    halo_cols = jnp.broadcast_to(halo_rows, (8, 2 * HALO)).T
    iota_h = lane_iota(HALO)
    for side in range(2):
        top, low = split_index(halo_cols[side * HALO:(side + 1) * HALO, :1])
        hsend[side] = dot(onehot(top, low, iota_h, VOX // L), own[...]).astype(BF)
    to_upper = remote(hsend.at[0], hrecv.at[0], halo_sems, 0, (above, rep))
    to_lower = remote(hsend.at[1], hrecv.at[1], halo_sems, 1, (below, rep))
    pl.semaphore_wait(barrier, N_SPACE - 1 + len(others))
    to_upper.start()
    to_lower.start()

    target = target_ref[...].astype(F32)
    child = jnp.floor((target + 0.5) * (1.0 / COARSE))
    cell = target - COARSE * child
    wdpad[...] = jnp.zeros_like(wdpad)
    for k in range(CHILDREN):
        wdpad[k * L:k * L + C, :C2] = wd_ref[k]
    for block in range(VOX // CHUNK):
        span = slice(block * CHUNK, (block + 1) * CHUNK)
        hits = jnp.concatenate(
            [onehot_of_row(cell[:, span] - b * CHUNK, CHUNK) for b in range(COARSE // CHUNK)], axis=0
        )
        picked = dot(cg_ref[0], hits).astype(BF)
        cgt[:, span] = picked
        every = dot(wdpad[:, :C2], picked)
        chosen = jnp.zeros((L, CHUNK), F32)
        for k in range(CHILDREN):
            chosen = jnp.where(child[:, span] == k, every[k * L:(k + 1) * L], chosen)
        back[span, :] = chosen.T
    for peer in range(N_SPACE):
        bsend[peer] = padded_rows(back[peer * CAP:(peer + 1) * CAP], PAD).astype(BF)
    brecv[me] = bsend[me]

    @pl.loop(1, N_SPACE)
    def _(d):
        swap_copy(bsend, brecv, swap_sems.at[0], swap_sems.at[1], (me + d) % N_SPACE, me, rep).start()

    wpad[...] = jnp.zeros_like(wpad)
    for k in range(OFFSETS):
        wpad[k * L:k * L + C, :C] = w_ref[k]
    rows = jnp.concatenate([kmap_ref[0], route_ref[...]], axis=0).astype(F32)
    index[...] = padded_rows(rows, L).T
    table[:, :L] = own[:HALF]
    table[:VOX - HALF, L:] = own[HALF:]
    to_upper.wait()
    to_lower.wait()
    table[VOX - HALF:VOX - HALF + HALO, L:] = jnp.where(me > 0, hrecv[0], jnp.zeros((), BF))
    table[VOX - HALF + HALO:, L:] = jnp.where(me < N_SPACE - 1, hrecv[1], jnp.zeros((), BF))

    iota_c = lane_iota(CHUNK)

    @pl.loop(0, VOX // CHUNK)
    def _(step):
        here = aligned(step, CHUNK)
        which = index[here, :]
        second = jnp.where(which >= HALF, 1.0, 0.0)
        top, low = split_index(which - HALF * second)
        for k in range(OFFSETS):
            both = dot(onehot(top[:, k:k + 1], low[:, k:k + 1], iota_c, HALF // L), table[...])
            picked = jnp.where(second[:, k:k + 1] > 0.5, both[:, L:], both[:, :L])
            gath[here, k * L:(k + 1) * L] = picked.astype(BF)
        pre = own[here, :].astype(F32) + dot(gath[here, :], wpad[...])
        pre_buf[here, :] = pre
        fine[here, :] = (pre * jax.nn.sigmoid(pre)).astype(BF)

    route = route_ref[...].astype(F32)
    group_rows = PEERS_AT_ONCE * CAP

    @pl.loop(0, N_SPACE // PEERS_AT_ONCE)
    def _(i):
        group = (me // PEERS_AT_ONCE + i) % (N_SPACE // PEERS_AT_ONCE)
        hits = onehot_of_row(route - (group * group_rows).astype(F32), group_rows)
        sent = dot(hits, fine[...])
        for j in range(PEERS_AT_ONCE):
            peer = group * PEERS_AT_ONCE + j
            fsend[peer] = padded_rows(sent[j * CAP:(j + 1) * CAP], PAD).astype(BF)

            @pl.when(peer != me)
            def _():
                swap_copy(fsend, frecv, swap_sems.at[2], swap_sems.at[3], peer, me, rep).start()

    frecv[me] = fsend[me]

    wait_swapped(bsend, brecv, swap_sems.at[0], swap_sems.at[1], me, rep, False)
    groups = N_SPACE // PEERS_AT_ONCE
    for group in range(groups):
        side, at = divmod(group, groups // 2)
        rettab[at * group_rows:(at + 1) * group_rows, side * L:(side + 1) * L] = (
            rows_of_group(brecv, group).astype(BF))
    acc[...] = jnp.zeros_like(acc)

    @pl.loop(0, VOX // CHUNK)
    def _(step):
        here = aligned(step, CHUNK)
        slot = index[here, :][:, OFFSETS:OFFSETS + 1]
        far = jnp.where(slot >= VOX // 2, 1.0, 0.0)
        top, low = split_index(slot - (VOX // 2) * far)
        both = dot(onehot(top, low, iota_c, VOX // 2 // L), rettab[...])
        fine_grad = jnp.where(far > 0.5, both[:, L:], both[:, :L])
        pre = pre_buf[here, :]
        sig = jax.nn.sigmoid(pre)
        pre_grad = fine_grad * sig * (1.0 + pre * (1.0 - sig))
        acc[...] += dot(pre_grad.T.astype(BF), gath[here, :])

    half = len(reduce_refs) // 2
    subm = Reducer(place, SUBM_SHARE, reduce_refs[:half])
    down = Reducer(place, DOWN_SHARE, reduce_refs[half:])
    for t, tile in enumerate(pack(lambda k, lo, hi: acc[:C, k * L + lo:k * L + hi], SUBM_TILES, OFFSETS)):
        subm.mine[t * C:(t + 1) * C] = tile
    subm.mine[SUBM_TILES * C:] = jnp.zeros((32 * SUBM_SHARE - SUBM_TILES * C, L), F32)
    subm.start_pair()
    subm.start_plane()

    wait_swapped(fsend, frecv, swap_sems.at[2], swap_sems.at[3], me, rep, False)
    child_cols = jnp.broadcast_to(child, (8, VOX)).T
    for group in range(groups):
        span = slice(group * group_rows, (group + 1) * group_rows)
        received = rows_of_group(frecv, group)
        kind = jnp.broadcast_to(child_cols[span, :1], (group_rows, L))
        for k in range(CHILDREN):
            cells_in[span, k * L:(k + 1) * L] = jnp.where(kind == k, received, 0.0).astype(BF)
    dacc[...] = dot(cgt[...], cells_in[...])
    for t, tile in enumerate(pack(lambda k, lo, hi: dacc[:, k * L + lo:k * L + hi], DOWN_TILES, CHILDREN)):
        down.mine[t * C2:(t + 1) * C2] = tile
    down.mine[DOWN_TILES * C2:] = jnp.zeros((32 * DOWN_SHARE - DOWN_TILES * C2, L), F32)
    down.start_pair()
    subm.start_column()
    down.start_plane()

    def coarse_block(block):
        hits = onehot_of_row(cell - block * CHUNK, CHUNK)
        cells = dot(hits, cells_in[...]).astype(BF)
        coarse_ref[0, :, block * CHUNK:(block + 1) * CHUNK] = dot(cells, wdpad[...]).T[:C2].astype(BF)

    coarse_block(0)
    subm.start_back()
    down.start_column()
    coarse_block(1)
    subm.start_over()
    down.start_back()
    coarse_block(2)
    down.start_over()
    subm.finish()

    def unpack(full, rows, k):
        parts = [full[t * rows:(t + 1) * rows, lo:hi].astype(F32) for t, lo, hi in tiles_of_block(k)]
        parts.append(jnp.zeros((rows, L - C), F32))
        return jnp.concatenate(parts, axis=1)

    for k in range(OFFSETS):
        sgrad_ref[k] = padded_rows(unpack(subm.full, C, k), L).T[:C, :C]
    down.finish()
    for k in range(CHILDREN):
        dgrad_ref[k] = padded_rows(unpack(down.full, C2, k), 2 * L).T[:C, :C2]
    wait_swapped(bsend, brecv, swap_sems.at[0], swap_sems.at[1], me, rep, True)
    wait_swapped(fsend, frecv, swap_sems.at[2], swap_sems.at[3], me, rep, True)
    subm.drain()
    down.drain()


def per_device(
    voxel_feats, kernel_map, halo_down, halo_up, route_slot, recv_target,
    subm_weight, down_weight, coarse_grad,
):
    vmem = pl.BlockSpec(memory_space=pltpu.VMEM)
    swap = pltpu.VMEM((N_SPACE, PAD, L), BF)
    return pl.pallas_call(
        step_kernel,
        out_shape=(
            jax.ShapeDtypeStruct((1, C2, COARSE), BF),
            jax.ShapeDtypeStruct((OFFSETS, C, C), F32),
            jax.ShapeDtypeStruct((CHILDREN, C, C2), F32),
        ),
        in_specs=[vmem] * 9,
        out_specs=(vmem,) * 3,
        scratch_shapes=[
            pltpu.VMEM((VOX, L), BF),
            pltpu.VMEM((HALF, 2 * L), BF),
            pltpu.VMEM((VOX // 2, 2 * L), BF),
            pltpu.VMEM((OFFSETS * L, L), BF),
            pltpu.VMEM((CHILDREN * L, 2 * L), BF),
            pltpu.VMEM((VOX, L), F32),
            pltpu.VMEM((VOX, OFFSETS * L), BF),
            pltpu.VMEM((VOX, L), F32),
            pltpu.VMEM((VOX, L), BF),
            pltpu.VMEM((L, OFFSETS * L), F32),
            pltpu.VMEM((C2, VOX), BF),
            pltpu.VMEM((VOX, L), F32),
            pltpu.VMEM((VOX, CHILDREN * L), BF),
            pltpu.VMEM((C2, CHILDREN * L), F32),
            pltpu.VMEM((2, HALO, L), BF),
            pltpu.VMEM((2, HALO, L), BF),
            swap, swap, swap, swap,
            pltpu.SemaphoreType.DMA((2, 2)),
            pltpu.SemaphoreType.DMA((4,)),
            *Reducer.scratch(SUBM_SHARE),
            *Reducer.scratch(DOWN_SHARE),
        ],
        compiler_params=pltpu.CompilerParams(
            collective_id=0, has_side_effects=True, vmem_limit_bytes=56 * MIB
        ),
        name="step",
    )(
        voxel_feats, kernel_map, halo_up, halo_down, route_slot, recv_target,
        subm_weight, down_weight, coarse_grad,
    )


def solution(mesh):
    in_specs = (
        P("rep", None, "space"),
        P("rep", None, "space"),
        P("rep", "space"),
        P("rep", "space"),
        P("rep", "space"),
        P("rep", "space"),
        P(),
        P(),
        P("rep", None, "space"),
    )
    out_specs = (P("rep", None, "space"), P(), P())
    return jax.shard_map(
        per_device, mesh=mesh, in_specs=in_specs, out_specs=out_specs, check_vma=False
    )
```

```python
import jax
import jax.numpy as jnp
from jax import lax
from jax.experimental import pallas as pl
from jax.experimental.pallas import tpu as pltpu
from jax.sharding import PartitionSpec as P

C = 96
C2 = 192
OFFSETS = 27
CHILDREN = 8
VOX = 1536
HALO = 384
COARSE = 768
CAP = 24
N_SPACE = 64
N_REP = 4
L = 128
PAD = 32
SUB = 512
QUADS = 7
CHUNK = 256
STEP = 384
PEERS_AT_ONCE = 8
MIB = 2**20
MESH = pl.DeviceIdType.MESH
BF = jnp.bfloat16
F32 = jnp.float32

SUBM_TILES = 21
DOWN_TILES = 6
SUBM_SHARE = 64
DOWN_SHARE = 48


def lane_iota(rows):
    return lax.broadcasted_iota(jnp.int32, (rows, L), 1).astype(F32).astype(BF)


def split_index(index):
    top = jnp.floor(index * (1.0 / L))
    return top.astype(BF), (index - L * top).astype(BF)


def onehot(top, low, iota, tiles):
    rows = iota.shape[0]
    zero = jnp.zeros((), BF)
    hit = jnp.where(jnp.broadcast_to(low, (rows, L)) == iota, jnp.ones((), BF), zero)
    tops = jnp.broadcast_to(top, (rows, L))
    return jnp.concatenate(
        [jnp.where(tops == jnp.asarray(t, BF), hit, zero) for t in range(tiles)], axis=1
    )


def onehot_of_row(row, rows):
    spread = jnp.broadcast_to(row, (rows, row.shape[1])).astype(BF)
    iota = lax.broadcasted_iota(jnp.int32, spread.shape, 0).astype(F32).astype(BF)
    return jnp.where(spread == iota, jnp.ones((), BF), jnp.zeros((), BF))


def padded_rows(x, rows):
    return jnp.concatenate([x, jnp.zeros((rows - x.shape[0], x.shape[1]), x.dtype)], axis=0)


def dot(a, b):
    return jnp.dot(a, b, preferred_element_type=F32)


def aligned(i, n):
    return pl.ds(pl.multiple_of(i * n, n), n)


def pack(blocks):
    piece = lambda k, lo, hi: blocks[:, k * L + lo:k * L + hi]
    return [
        jnp.concatenate([piece(0, 0, C), piece(1, 0, 32)], axis=1),
        jnp.concatenate([piece(1, 32, C), piece(2, 0, 64)], axis=1),
        jnp.concatenate([piece(2, 64, C), piece(3, 0, C)], axis=1),
    ]


def tiles_of_block(k):
    q, r = divmod(k, 4)
    pieces = []
    if r:
        pieces.append((3 * q + r - 1, L - 32 * r, L))
    if r < 3:
        pieces.append((3 * q + r, 0, C - 32 * r))
    return pieces


class Place:
    def __init__(self):
        space, y = lax.axis_index("space"), lax.axis_index("rep")
        core, z, x = space % 2, (space // 2) % 8, space // 16
        at = lambda xx, zz, cc: (xx * 8 + zz) * 2 + cc
        self.space, self.rep, self.core, self.z = space, y, core, z
        self.partner = (at(x, z, 1 - core), y)
        self.plane = [(at((x + d // 4) % 4, z, core), (y + d % 4) % 4) for d in range(16)]
        self.plane_to = [((x + d // 4) % 4) * 4 + (y + d % 4) % 4 for d in range(16)]
        self.plane_from = [((x + 4 - d // 4) % 4) * 4 + (y + 4 - d % 4) % 4 for d in range(16)]
        self.column = [(at(x, (z + d) % 8, core), y) for d in range(8)]
        self.column_from = [(z + 8 - d) % 8 for d in range(8)]


def remote(src, dst, sems, i, peer):
    return pltpu.make_async_remote_copy(
        src_ref=src, dst_ref=dst, send_sem=sems.at[0, i], recv_sem=sems.at[1, i],
        device_id=peer, device_id_type=MESH,
    )


class Reducer:
    @staticmethod
    def scratch(share):
        return [
            pltpu.VMEM((32 * share, L), F32),
            pltpu.VMEM((16 * share, L), BF),
            pltpu.VMEM((16 * share, L), BF),
            pltpu.VMEM((16, share, L), BF),
            pltpu.VMEM((16, share, L), BF),
            pltpu.VMEM((share, L), BF),
            pltpu.VMEM((8, share, L), BF),
            pltpu.VMEM((32 * share, L), BF),
            pltpu.SemaphoreType.DMA((2, 16)),
            pltpu.SemaphoreType.DMA((2, 16)),
            pltpu.SemaphoreType.DMA((2, 8)),
            pltpu.SemaphoreType.DMA((2, 16)),
            pltpu.SemaphoreType.DMA((2, 16)),
        ]

    def __init__(self, place, share, refs):
        self.place, self.share = place, share
        (self.mine, self.theirs, self.pair, self.psend, self.plane, self.zsend, self.column, self.full,
         self.pair_sems, self.plane_sems, self.z_sems, self.back_sems, self.over_sems) = refs
        self.sends = []

    def go(self, copy):
        copy.start()
        self.sends.append(copy)
        return copy

    def start_pair(self):
        p, n = self.place, self.share
        self.theirs[...] = self.mine[aligned(1 - p.core, 16 * n)].astype(BF)
        self.in_pair = []
        for d in range(16):
            at = aligned(p.plane_to[d], n)
            self.in_pair.append(self.go(
                remote(self.theirs.at[at], self.pair.at[at], self.pair_sems, d, p.partner)))

    def start_plane(self):
        p, n = self.place, self.share
        self.in_plane = []
        for d in list(range(1, 16)) + [0]:
            self.in_pair[d].wait_recv()
            both = (self.mine[aligned(p.core * 16 + p.plane_to[d], n)]
                    + self.pair[aligned(p.plane_to[d], n)].astype(F32))
            if d:
                self.psend[d] = both.astype(BF)
                self.in_plane.append(self.go(
                    remote(self.psend.at[d], self.plane.at[d], self.plane_sems, d, p.plane[d])))
        self.total = both

    def start_column(self):
        p = self.place
        total = self.total
        for d in range(1, 16):
            self.in_plane[d - 1].wait_recv()
            total += self.plane[d].astype(F32)
        self.zsend[...] = total.astype(BF)
        self.in_column = []
        for d in range(1, 8):
            self.in_column.append(self.go(
                remote(self.zsend, self.column.at[p.z], self.z_sems, d, p.column[d])))
        self.column[p.z] = total.astype(BF)

    def start_back(self):
        p, n = self.place, self.share
        for copy in self.in_column:
            copy.wait_recv()
        total = self.column[0].astype(F32)
        for z in range(1, 8):
            total += self.column[z].astype(F32)
        here = aligned(p.core * 16 + p.plane_to[0], n)
        self.full[here] = total.astype(BF)
        self.in_back = []
        for d in range(1, 16):
            self.in_back.append(self.go(
                remote(self.full.at[here], self.full.at[here], self.back_sems, d, p.plane[d])))

    def start_over(self):
        p, n = self.place, self.share
        self.in_over = []
        for d in range(16):
            if d:
                self.in_back[d - 1].wait_recv()
            at = aligned(p.core * 16 + p.plane_from[d], n)
            self.in_over.append(self.go(
                remote(self.full.at[at], self.full.at[at], self.over_sems, d, p.partner)))

    def finish(self):
        for copy in self.in_over:
            copy.wait_recv()

    def drain(self):
        for copy in self.sends:
            copy.wait_send()


def swap_copy(src, dst, send_sem, recv_sem, peer, me, rep):
    return pltpu.make_async_remote_copy(
        src_ref=src.at[peer], dst_ref=dst.at[me], send_sem=send_sem, recv_sem=recv_sem,
        device_id=(peer, rep), device_id_type=MESH,
    )


def wait_swapped(src, dst, send_sem, recv_sem, me, rep, sent):
    others = pl.ds(0, N_SPACE - 1)
    copies = pltpu.make_async_remote_copy(
        src_ref=src.at[others], dst_ref=dst.at[others], send_sem=send_sem, recv_sem=recv_sem,
        device_id=((me + 1) % N_SPACE, rep), device_id_type=MESH,
    )
    if sent:
        copies.wait_send()
    else:
        copies.wait_recv()


def rows_of_group(ref, group):
    return jnp.concatenate(
        [ref[group * PEERS_AT_ONCE + i].astype(F32)[:CAP] for i in range(PEERS_AT_ONCE)], axis=0
    )


def step_kernel(
    feats_ref, kmap_ref, up_ref, down_ref, route_ref, target_ref, w_ref, wd_ref, cg_ref,
    coarse_ref, sgrad_ref, dgrad_ref,
    ordered, own, table, wpad, wdpad, gath, pre_buf, pre_grads, cgt, back, cells_in,
    hsend, hrecv, bsend, brecv, fsend, frecv, halo_sems, swap_sems, *reduce_refs,
):
    place = Place()
    me, rep = place.space, place.rep
    above, below = (me + 1) % N_SPACE, (me + N_SPACE - 1) % N_SPACE
    barrier = pltpu.get_barrier_semaphore()

    @pl.loop(1, N_SPACE)
    def _(d):
        pl.semaphore_signal(barrier, inc=1, device_id=((me + d) % N_SPACE, rep), device_id_type=MESH)

    others = [place.plane[d] for d in range(16) if d % 4]
    for peer in others:
        pl.semaphore_signal(barrier, inc=1, device_id=peer, device_id_type=MESH)

    own[...] = padded_rows(feats_ref[0].astype(F32), L).T.astype(BF)
    halo_rows = jnp.concatenate([up_ref[...], down_ref[...]], axis=1).astype(F32)
    halo_cols = jnp.broadcast_to(halo_rows, (8, 2 * HALO)).T
    iota_h = lane_iota(HALO)
    for side in range(2):
        top, low = split_index(halo_cols[side * HALO:(side + 1) * HALO, :1])
        hsend[side] = dot(onehot(top, low, iota_h, VOX // L), own[...]).astype(BF)

    target = target_ref[...].astype(F32)
    child = jnp.floor((target + 0.5) * (1.0 / COARSE))
    cell = target - COARSE * child
    wdpad[...] = jnp.zeros_like(wdpad)
    for k in range(CHILDREN):
        wdpad[k * L:k * L + C, :C2] = wd_ref[k]
    for block in range(VOX // CHUNK):
        span = slice(block * CHUNK, (block + 1) * CHUNK)
        hits = jnp.concatenate(
            [onehot_of_row(cell[:, span] - b * CHUNK, CHUNK) for b in range(COARSE // CHUNK)], axis=0
        )
        picked = dot(cg_ref[0], hits).astype(BF)
        cgt[:, span] = picked
        every = dot(wdpad[:, :C2], picked)
        chosen = jnp.zeros((L, CHUNK), F32)
        for k in range(CHILDREN):
            chosen = jnp.where(child[:, span] == k, every[k * L:(k + 1) * L], chosen)
        back[span, :] = chosen.T
    for peer in range(N_SPACE):
        bsend[peer] = padded_rows(back[peer * CAP:(peer + 1) * CAP], PAD).astype(BF)
    brecv[me] = bsend[me]

    neighbours = kmap_ref[0].astype(F32)
    sub = jnp.floor(neighbours * (1.0 / SUB))
    rest = neighbours - SUB * sub
    tile = jnp.floor(rest * (1.0 / L))
    parts = [padded_rows(x, PAD) for x in (sub, tile, rest - L * tile)]
    ordered[:, :L] = padded_rows(jnp.concatenate(parts, axis=0), L).T.astype(BF)
    ordered[:, L:] = own[...]

    to_upper = remote(hsend.at[0], hrecv.at[0], halo_sems, 0, (above, rep))
    to_lower = remote(hsend.at[1], hrecv.at[1], halo_sems, 1, (below, rep))
    pl.semaphore_wait(barrier, N_SPACE - 1 + len(others))
    to_upper.start()
    to_lower.start()

    @pl.loop(1, N_SPACE)
    def _(d):
        swap_copy(bsend, brecv, swap_sems.at[0], swap_sems.at[1], (me + d) % N_SPACE, me, rep).start()

    wpad[...] = jnp.zeros_like(wpad)
    for k in range(OFFSETS):
        wpad[k * L:k * L + C, :C] = w_ref[k]
    for j in range(3):
        table[:, j * L:(j + 1) * L] = own[j * SUB:(j + 1) * SUB]
    to_upper.wait()
    to_lower.wait()
    table[:HALO, 3 * L:] = jnp.where(me > 0, hrecv[0], jnp.zeros((), BF))
    upper = jnp.where(me < N_SPACE - 1, hrecv[1], jnp.zeros((), BF))
    table[HALO:, 3 * L:] = upper[:SUB - HALO]
    last = upper[SUB - HALO:].astype(F32)
    lane = lax.broadcasted_iota(jnp.int32, last.shape, 1)
    for j in range(3):
        spare = pltpu.roll(last, C - 32 * j, 1)
        kept = own[j * SUB:j * SUB + last.shape[0]].astype(F32)
        table[:last.shape[0], j * L:(j + 1) * L] = jnp.where(lane < C, kept, spare).astype(BF)

    iota_s = lane_iota(STEP)
    lane_s = lax.broadcasted_iota(jnp.int32, (STEP, L), 1)
    route = route_ref[...].astype(F32)
    peers = STEP // CAP

    @pl.loop(0, VOX // STEP)
    def _(i):
        turn = (me // peers + i) % (VOX // STEP)
        here = aligned(turn, STEP)
        start = (turn * STEP).astype(F32)
        hits = jnp.concatenate(
            [onehot_of_row(route - (start + off), STEP // 2) for off in (0.0, STEP / 2.0)], axis=0
        )
        mine = dot(hits, ordered[...])
        which = mine[:, :L].astype(BF)
        for k in range(OFFSETS):
            hot = onehot(which[:, PAD + k:PAD + k + 1], which[:, 2 * PAD + k:2 * PAD + k + 1], iota_s, SUB // L)
            every = dot(hot, table[...])
            blocks = [every[:, j * L:(j + 1) * L] for j in range(4)]
            spare = jnp.where(
                lane_s < 32, pltpu.roll(blocks[0], 32, 1),
                jnp.where(lane_s < 64, pltpu.roll(blocks[1], 64, 1), pltpu.roll(blocks[2], 96, 1)),
            )
            kind = jnp.broadcast_to(mine[:, k:k + 1], (STEP, L))
            picked = blocks[0]
            for j, block in enumerate(blocks[1:] + [spare]):
                picked = jnp.where(kind == j + 1, block, picked)
            gath[here, k * L:(k + 1) * L] = picked.astype(BF)
        pre = mine[:, L:] + dot(gath[here, :OFFSETS * L], wpad[...])
        pre_buf[here, :] = pre
        fine = pre * jax.nn.sigmoid(pre)
        for j in range(peers):
            peer = turn * peers + j
            fsend[peer] = padded_rows(fine[j * CAP:(j + 1) * CAP], PAD).astype(BF)

            @pl.when(peer != me)
            def _():
                swap_copy(fsend, frecv, swap_sems.at[2], swap_sems.at[3], peer, me, rep).start()

    frecv[me] = fsend[me]

    half = len(reduce_refs) // 2
    subm = Reducer(place, SUBM_SHARE, reduce_refs[:half])
    down = Reducer(place, DOWN_SHARE, reduce_refs[half:])
    groups = N_SPACE // PEERS_AT_ONCE
    group_rows = PEERS_AT_ONCE * CAP
    wait_swapped(bsend, brecv, swap_sems.at[0], swap_sems.at[1], me, rep, False)
    for step in range(VOX // STEP):
        span = slice(step * STEP, (step + 1) * STEP)
        fine_grad = jnp.concatenate([rows_of_group(brecv, 2 * step + i) for i in range(2)], axis=0)
        pre = pre_buf[span, :]
        sig = jax.nn.sigmoid(pre)
        pre_grad = fine_grad * sig * (1.0 + pre * (1.0 - sig))
        pre_grads[:, span] = pre_grad.T.astype(BF)
    gath[:, OFFSETS * L:] = jnp.zeros((VOX, L), BF)
    for quad in range(QUADS):
        grads = dot(pre_grads[...], gath[:, quad * 4 * L:(quad + 1) * 4 * L])[:C]
        for i, packed in enumerate(pack(grads)):
            subm.mine[(3 * quad + i) * C:(3 * quad + i + 1) * C] = packed
    subm.mine[SUBM_TILES * C:] = jnp.zeros((32 * SUBM_SHARE - SUBM_TILES * C, L), F32)
    subm.start_pair()
    subm.start_plane()

    wait_swapped(fsend, frecv, swap_sems.at[2], swap_sems.at[3], me, rep, False)
    child_cols = jnp.broadcast_to(child, (8, VOX)).T
    for group in range(groups):
        span = slice(group * group_rows, (group + 1) * group_rows)
        received = rows_of_group(frecv, group)
        kind = jnp.broadcast_to(child_cols[span, :1], (group_rows, L))
        for k in range(CHILDREN):
            cells_in[span, k * L:(k + 1) * L] = jnp.where(kind == k, received, 0.0).astype(BF)
    for quad in range(CHILDREN // 4):
        grads = dot(cgt[...], cells_in[:, quad * 4 * L:(quad + 1) * 4 * L])
        for i, packed in enumerate(pack(grads)):
            down.mine[(3 * quad + i) * C2:(3 * quad + i + 1) * C2] = packed
    down.mine[DOWN_TILES * C2:] = jnp.zeros((32 * DOWN_SHARE - DOWN_TILES * C2, L), F32)
    down.start_pair()
    subm.start_column()
    down.start_plane()

    def coarse_block(block):
        hits = onehot_of_row(cell - block * CHUNK, CHUNK)
        cells = dot(hits, cells_in[...]).astype(BF)
        coarse_ref[0, :, block * CHUNK:(block + 1) * CHUNK] = dot(cells, wdpad[...]).T[:C2].astype(BF)

    coarse_block(0)
    subm.start_back()
    down.start_column()
    coarse_block(1)
    subm.start_over()
    down.start_back()
    coarse_block(2)
    down.start_over()
    subm.finish()

    def unpack(full, rows, k):
        parts = [full[t * rows:(t + 1) * rows, lo:hi].astype(F32) for t, lo, hi in tiles_of_block(k)]
        parts.append(jnp.zeros((rows, L - C), F32))
        return jnp.concatenate(parts, axis=1)

    for k in range(OFFSETS):
        sgrad_ref[k] = padded_rows(unpack(subm.full, C, k), L).T[:C, :C]
    down.finish()
    for k in range(CHILDREN):
        dgrad_ref[k] = padded_rows(unpack(down.full, C2, k), 2 * L).T[:C, :C2]
    wait_swapped(bsend, brecv, swap_sems.at[0], swap_sems.at[1], me, rep, True)
    wait_swapped(fsend, frecv, swap_sems.at[2], swap_sems.at[3], me, rep, True)
    subm.drain()
    down.drain()


def per_device(
    voxel_feats, kernel_map, halo_down, halo_up, route_slot, recv_target,
    subm_weight, down_weight, coarse_grad,
):
    vmem = pl.BlockSpec(memory_space=pltpu.VMEM)
    swap = pltpu.VMEM((N_SPACE, PAD, L), BF)
    return pl.pallas_call(
        step_kernel,
        out_shape=(
            jax.ShapeDtypeStruct((1, C2, COARSE), BF),
            jax.ShapeDtypeStruct((OFFSETS, C, C), F32),
            jax.ShapeDtypeStruct((CHILDREN, C, C2), F32),
        ),
        in_specs=[vmem] * 9,
        out_specs=(vmem,) * 3,
        scratch_shapes=[
            pltpu.VMEM((VOX, 2 * L), BF),
            pltpu.VMEM((VOX, L), BF),
            pltpu.VMEM((SUB, 4 * L), BF),
            pltpu.VMEM((OFFSETS * L, L), BF),
            pltpu.VMEM((CHILDREN * L, 2 * L), BF),
            pltpu.VMEM((VOX, QUADS * 4 * L), BF),
            pltpu.VMEM((VOX, L), F32),
            pltpu.VMEM((L, VOX), BF),
            pltpu.VMEM((C2, VOX), BF),
            pltpu.VMEM((VOX, L), F32),
            pltpu.VMEM((VOX, CHILDREN * L), BF),
            pltpu.VMEM((2, HALO, L), BF),
            pltpu.VMEM((2, HALO, L), BF),
            swap, swap, swap, swap,
            pltpu.SemaphoreType.DMA((2, 2)),
            pltpu.SemaphoreType.DMA((4,)),
            *Reducer.scratch(SUBM_SHARE),
            *Reducer.scratch(DOWN_SHARE),
        ],
        compiler_params=pltpu.CompilerParams(
            collective_id=0, has_side_effects=True, vmem_limit_bytes=56 * MIB
        ),
        name="step",
    )(
        voxel_feats, kernel_map, halo_up, halo_down, route_slot, recv_target,
        subm_weight, down_weight, coarse_grad,
    )


def solution(mesh):
    in_specs = (
        P("rep", None, "space"),
        P("rep", None, "space"),
        P("rep", "space"),
        P("rep", "space"),
        P("rep", "space"),
        P("rep", "space"),
        P(),
        P(),
        P("rep", None, "space"),
    )
    out_specs = (P("rep", None, "space"), P(), P())
    return jax.shard_map(
        per_device, mesh=mesh, in_specs=in_specs, out_specs=out_specs, check_vma=False
    )
```

```python
import jax
import jax.numpy as jnp
from jax import lax
from jax.experimental import pallas as pl
from jax.experimental.pallas import tpu as pltpu
from jax.sharding import PartitionSpec as P

C = 96
C2 = 192
OFFSETS = 27
CHILDREN = 8
VOX = 1536
HALO = 384
COARSE = 768
CAP = 24
N_SPACE = 64
N_REP = 4
L = 128
PAD = 32
OWN_SUB = 768
RIM_SUB = 256
QUADS = 7
CHUNK = 256
STEP = 384
SEND_STEP = 192
EARLY = 2
PEERS_AT_ONCE = 8
MIB = 2**20
MESH = pl.DeviceIdType.MESH
BF = jnp.bfloat16
F32 = jnp.float32

SUBM_TILES = 21
DOWN_TILES = 6
SUBM_SHARE = 64
DOWN_SHARE = 48


def lane_iota(rows):
    return lax.broadcasted_iota(jnp.int32, (rows, L), 1).astype(F32).astype(BF)


def split_index(index):
    top = jnp.floor(index * (1.0 / L))
    return top.astype(BF), (index - L * top).astype(BF)


def onehot(top, low, iota, tiles):
    rows = iota.shape[0]
    zero = jnp.zeros((), BF)
    hit = jnp.where(jnp.broadcast_to(low, (rows, L)) == iota, jnp.ones((), BF), zero)
    tops = jnp.broadcast_to(top, (rows, L))
    return jnp.concatenate(
        [jnp.where(tops == jnp.asarray(t, BF), hit, zero) for t in range(tiles)], axis=1
    )


def onehot_of_row(row, rows):
    spread = jnp.broadcast_to(row, (rows, row.shape[1])).astype(BF)
    iota = lax.broadcasted_iota(jnp.int32, spread.shape, 0).astype(F32).astype(BF)
    return jnp.where(spread == iota, jnp.ones((), BF), jnp.zeros((), BF))


def padded_rows(x, rows):
    return jnp.concatenate([x, jnp.zeros((rows - x.shape[0], x.shape[1]), x.dtype)], axis=0)


def dot(a, b):
    return jnp.dot(a, b, preferred_element_type=F32)


def aligned(i, n):
    return pl.ds(pl.multiple_of(i * n, n), n)


def pack(blocks):
    piece = lambda k, lo, hi: blocks[:, k * L + lo:k * L + hi]
    return [
        jnp.concatenate([piece(0, 0, C), piece(1, 0, 32)], axis=1),
        jnp.concatenate([piece(1, 32, C), piece(2, 0, 64)], axis=1),
        jnp.concatenate([piece(2, 64, C), piece(3, 0, C)], axis=1),
    ]


def tiles_of_block(k):
    q, r = divmod(k, 4)
    pieces = []
    if r:
        pieces.append((3 * q + r - 1, L - 32 * r, L))
    if r < 3:
        pieces.append((3 * q + r, 0, C - 32 * r))
    return pieces


class Place:
    def __init__(self):
        space, y = lax.axis_index("space"), lax.axis_index("rep")
        core, z, x = space % 2, (space // 2) % 8, space // 16
        at = lambda xx, zz, cc: (xx * 8 + zz) * 2 + cc
        self.space, self.rep, self.core, self.z = space, y, core, z
        self.partner = (at(x, z, 1 - core), y)
        self.plane = [(at((x + d // 4) % 4, z, core), (y + d % 4) % 4) for d in range(16)]
        self.plane_to = [((x + d // 4) % 4) * 4 + (y + d % 4) % 4 for d in range(16)]
        self.plane_from = [((x + 4 - d // 4) % 4) * 4 + (y + 4 - d % 4) % 4 for d in range(16)]
        self.column = [(at(x, (z + d) % 8, core), y) for d in range(8)]
        self.column_from = [(z + 8 - d) % 8 for d in range(8)]


def remote(src, dst, sems, i, peer):
    return pltpu.make_async_remote_copy(
        src_ref=src, dst_ref=dst, send_sem=sems.at[0, i], recv_sem=sems.at[1, i],
        device_id=peer, device_id_type=MESH,
    )


class Reducer:
    @staticmethod
    def scratch(share):
        return [
            pltpu.VMEM((32 * share, L), F32),
            pltpu.VMEM((16 * share, L), BF),
            pltpu.VMEM((16 * share, L), BF),
            pltpu.VMEM((16, share, L), BF),
            pltpu.VMEM((16, share, L), BF),
            pltpu.VMEM((share, L), BF),
            pltpu.VMEM((8, share, L), BF),
            pltpu.VMEM((32 * share, L), BF),
            pltpu.SemaphoreType.DMA((2, 16)),
            pltpu.SemaphoreType.DMA((2, 16)),
            pltpu.SemaphoreType.DMA((2, 8)),
            pltpu.SemaphoreType.DMA((2, 16)),
            pltpu.SemaphoreType.DMA((2, 16)),
        ]

    def __init__(self, place, share, refs):
        self.place, self.share = place, share
        (self.mine, self.theirs, self.pair, self.psend, self.plane, self.zsend, self.column, self.full,
         self.pair_sems, self.plane_sems, self.z_sems, self.back_sems, self.over_sems) = refs
        self.sends = []

    def go(self, copy):
        copy.start()
        self.sends.append(copy)
        return copy

    def start_pair(self):
        p, n = self.place, self.share
        self.theirs[...] = self.mine[aligned(1 - p.core, 16 * n)].astype(BF)
        self.in_pair = []
        for d in range(16):
            at = aligned(p.plane_to[d], n)
            self.in_pair.append(self.go(
                remote(self.theirs.at[at], self.pair.at[at], self.pair_sems, d, p.partner)))

    def start_plane(self):
        p, n = self.place, self.share
        self.in_plane = []
        for d in list(range(1, 16)) + [0]:
            self.in_pair[d].wait_recv()
            both = (self.mine[aligned(p.core * 16 + p.plane_to[d], n)]
                    + self.pair[aligned(p.plane_to[d], n)].astype(F32))
            if d:
                self.psend[d] = both.astype(BF)
                self.in_plane.append(self.go(
                    remote(self.psend.at[d], self.plane.at[d], self.plane_sems, d, p.plane[d])))
        self.total = both

    def start_column(self):
        p = self.place
        total = self.total
        for d in range(1, 16):
            self.in_plane[d - 1].wait_recv()
            total += self.plane[d].astype(F32)
        self.zsend[...] = total.astype(BF)
        self.in_column = []
        for d in range(1, 8):
            self.in_column.append(self.go(
                remote(self.zsend, self.column.at[p.z], self.z_sems, d, p.column[d])))
        self.column[p.z] = total.astype(BF)

    def start_back(self):
        p, n = self.place, self.share
        for copy in self.in_column:
            copy.wait_recv()
        total = self.column[0].astype(F32)
        for z in range(1, 8):
            total += self.column[z].astype(F32)
        here = aligned(p.core * 16 + p.plane_to[0], n)
        self.full[here] = total.astype(BF)
        self.in_back = []
        for d in range(1, 16):
            self.in_back.append(self.go(
                remote(self.full.at[here], self.full.at[here], self.back_sems, d, p.plane[d])))

    def start_over(self):
        p, n = self.place, self.share
        self.in_over = []
        for d in range(16):
            if d:
                self.in_back[d - 1].wait_recv()
            at = aligned(p.core * 16 + p.plane_from[d], n)
            self.in_over.append(self.go(
                remote(self.full.at[at], self.full.at[at], self.over_sems, d, p.partner)))

    def finish(self):
        for copy in self.in_over:
            copy.wait_recv()

    def drain(self):
        for copy in self.sends:
            copy.wait_send()


def swap_copy(src, dst, send_sem, recv_sem, peer, me, rep):
    return pltpu.make_async_remote_copy(
        src_ref=src.at[peer], dst_ref=dst.at[me], send_sem=send_sem, recv_sem=recv_sem,
        device_id=(peer, rep), device_id_type=MESH,
    )


def wait_swapped(src, dst, send_sem, recv_sem, me, rep, sent):
    others = pl.ds(0, N_SPACE - 1)
    copies = pltpu.make_async_remote_copy(
        src_ref=src.at[others], dst_ref=dst.at[others], send_sem=send_sem, recv_sem=recv_sem,
        device_id=((me + 1) % N_SPACE, rep), device_id_type=MESH,
    )
    if sent:
        copies.wait_send()
    else:
        copies.wait_recv()


def rows_of_group(ref, group):
    return jnp.concatenate(
        [ref[group * PEERS_AT_ONCE + i].astype(F32)[:CAP] for i in range(PEERS_AT_ONCE)], axis=0
    )


def step_kernel(
    feats_ref, kmap_ref, up_ref, down_ref, route_ref, target_ref, w_ref, wd_ref, cg_ref,
    coarse_ref, subm_ref, dsum_ref,
    ordered, own, table, rim, which_buf, wpad, wdpad, gath, pre_buf, pre_grads, cgt, back, cells_in,
    hsend, hrecv, bsend, brecv, fsend, frecv, halo_sems, swap_sems, *reduce_refs,
):
    place = Place()
    me, rep = place.space, place.rep
    above, below = (me + 1) % N_SPACE, (me + N_SPACE - 1) % N_SPACE
    barrier = pltpu.get_barrier_semaphore()

    @pl.loop(1, N_SPACE)
    def _(d):
        pl.semaphore_signal(barrier, inc=1, device_id=((me + d) % N_SPACE, rep), device_id_type=MESH)

    others = [place.plane[d] for d in range(16) if d % 4]
    for peer in others:
        pl.semaphore_signal(barrier, inc=1, device_id=peer, device_id_type=MESH)

    own[...] = padded_rows(feats_ref[0].astype(F32), L).T.astype(BF)
    halo_rows = jnp.concatenate([up_ref[...], down_ref[...]], axis=1).astype(F32)
    halo_cols = jnp.broadcast_to(halo_rows, (8, 2 * HALO)).T
    iota_h = lane_iota(HALO)
    for side in range(2):
        top, low = split_index(halo_cols[side * HALO:(side + 1) * HALO, :1])
        hsend[side] = dot(onehot(top, low, iota_h, VOX // L), own[...]).astype(BF)

    target = target_ref[...].astype(F32)
    child = jnp.floor((target + 0.5) * (1.0 / COARSE))
    cell = target - COARSE * child
    wdpad[...] = jnp.zeros_like(wdpad)
    for k in range(CHILDREN):
        wdpad[k * L:k * L + C, :C2] = wd_ref[k]
    for block in range(VOX // CHUNK):
        span = slice(block * CHUNK, (block + 1) * CHUNK)
        hits = jnp.concatenate(
            [onehot_of_row(cell[:, span] - b * CHUNK, CHUNK) for b in range(COARSE // CHUNK)], axis=0
        )
        picked = dot(cg_ref[0], hits).astype(BF)
        cgt[:, span] = picked
        every = dot(wdpad[:, :C2], picked)
        chosen = jnp.zeros((L, CHUNK), F32)
        for k in range(CHILDREN):
            chosen = jnp.where(child[:, span] == k, every[k * L:(k + 1) * L], chosen)
        back[span, :] = chosen.T
    for peer in range(N_SPACE):
        bsend[peer] = padded_rows(back[peer * CAP:(peer + 1) * CAP], PAD).astype(BF)
    brecv[me] = bsend[me]

    neighbours = jnp.concatenate([kmap_ref[k] for k in range(OFFSETS)], axis=0).astype(F32)
    tile = jnp.floor(neighbours * (1.0 / L))
    parts = [padded_rows(x, PAD) for x in (tile, neighbours - L * tile)]
    ordered[:, :L] = padded_rows(jnp.concatenate(parts, axis=0), L).T.astype(BF)
    ordered[:, L:] = own[...]
    for j in range(2):
        table[:, j * L:(j + 1) * L] = own[j * OWN_SUB:(j + 1) * OWN_SUB]
    wpad[...] = jnp.zeros_like(wpad)
    for k in range(OFFSETS):
        wpad[k * L:k * L + C, :C] = w_ref[k]
    route = route_ref[...].astype(F32)
    iota_s = lane_iota(STEP)
    own_tiles = OWN_SUB // L

    def gather_own(turn):
        here = aligned(turn, STEP)
        start = (turn * STEP).astype(F32)
        hits = jnp.concatenate(
            [onehot_of_row(route - (start + off), STEP // 2) for off in (0.0, STEP / 2.0)], axis=0
        )
        mine = dot(hits, ordered[...])
        which = mine[:, :L]
        which_buf[here, :] = which
        pre_buf[here, :] = mine[:, L:]
        second = jnp.where(which >= own_tiles, 1.0, 0.0)
        top, low = (which - own_tiles * second).astype(BF), which.astype(BF)
        for k in range(OFFSETS):
            hot = onehot(top[:, k:k + 1], low[:, PAD + k:PAD + k + 1], iota_s, own_tiles)
            both = dot(hot, table[...])
            picked = jnp.where(second[:, k:k + 1] > 0.5, both[:, L:], both[:, :L])
            gath[here, k * L:(k + 1) * L] = picked.astype(BF)

    pl.loop(0, EARLY)(gather_own)

    to_upper = remote(hsend.at[0], hrecv.at[0], halo_sems, 0, (above, rep))
    to_lower = remote(hsend.at[1], hrecv.at[1], halo_sems, 1, (below, rep))
    pl.semaphore_wait(barrier, N_SPACE - 1 + len(others))
    to_upper.start()
    to_lower.start()

    @pl.loop(1, N_SPACE)
    def _(d):
        swap_copy(bsend, brecv, swap_sems.at[0], swap_sems.at[1], (me + d) % N_SPACE, me, rep).start()

    pl.loop(EARLY, VOX // STEP)(gather_own)

    to_upper.wait()
    to_lower.wait()
    lower = jnp.where(me > 0, hrecv[0], jnp.zeros((), BF))
    upper = jnp.where(me < N_SPACE - 1, hrecv[1], jnp.zeros((), BF))
    rim[:, :L] = lower[:RIM_SUB]
    rim[:HALO - RIM_SUB, L:2 * L] = lower[RIM_SUB:]
    rim[HALO - RIM_SUB:, L:2 * L] = upper[:2 * RIM_SUB - HALO]
    rim[:, 2 * L:] = upper[2 * RIM_SUB - HALO:]

    iota_r = lane_iota(SEND_STEP)
    peers = SEND_STEP // CAP
    rim_tiles = RIM_SUB // L

    @pl.loop(0, VOX // SEND_STEP)
    def _(i):
        turn = (me // peers + i) % (VOX // SEND_STEP)
        here = aligned(turn, SEND_STEP)
        which = which_buf[here, :]
        beyond = which - VOX // L
        kind = jnp.floor(beyond * (1.0 / rim_tiles))
        top, low = (beyond - rim_tiles * kind).astype(BF), which.astype(BF)
        for k in range(OFFSETS):
            lanes = slice(k * L, (k + 1) * L)
            hot = onehot(top[:, k:k + 1], low[:, PAD + k:PAD + k + 1], iota_r, rim_tiles)
            every = dot(hot, rim[...])
            kinds = jnp.broadcast_to(kind[:, k:k + 1], (SEND_STEP, L))
            picked = gath[here, lanes].astype(F32)
            for j in range(3):
                picked = jnp.where(kinds == j, every[:, j * L:(j + 1) * L], picked)
            gath[here, lanes] = picked.astype(BF)
        pre = pre_buf[here, :] + dot(gath[here, :OFFSETS * L], wpad[...])
        pre_buf[here, :] = pre
        fine = pre * jax.nn.sigmoid(pre)
        for j in range(peers):
            peer = turn * peers + j
            fsend[peer] = padded_rows(fine[j * CAP:(j + 1) * CAP], PAD).astype(BF)

            @pl.when(peer != me)
            def _():
                swap_copy(fsend, frecv, swap_sems.at[2], swap_sems.at[3], peer, me, rep).start()

    frecv[me] = fsend[me]

    half = len(reduce_refs) // 2
    subm = Reducer(place, SUBM_SHARE, reduce_refs[:half])
    down = Reducer(place, DOWN_SHARE, reduce_refs[half:])
    groups = N_SPACE // PEERS_AT_ONCE
    group_rows = PEERS_AT_ONCE * CAP
    wait_swapped(bsend, brecv, swap_sems.at[0], swap_sems.at[1], me, rep, False)
    for step in range(VOX // STEP):
        span = slice(step * STEP, (step + 1) * STEP)
        fine_grad = jnp.concatenate([rows_of_group(brecv, 2 * step + i) for i in range(2)], axis=0)
        pre = pre_buf[span, :]
        sig = jax.nn.sigmoid(pre)
        pre_grad = fine_grad * sig * (1.0 + pre * (1.0 - sig))
        pre_grads[:, span] = pre_grad.T.astype(BF)
    gath[:, OFFSETS * L:] = jnp.zeros((VOX, L), BF)
    for quad in range(QUADS):
        grads = dot(pre_grads[...], gath[:, quad * 4 * L:(quad + 1) * 4 * L])[:C]
        for i, packed in enumerate(pack(grads)):
            subm.mine[(3 * quad + i) * C:(3 * quad + i + 1) * C] = packed
    subm.mine[SUBM_TILES * C:] = jnp.zeros((32 * SUBM_SHARE - SUBM_TILES * C, L), F32)
    subm.start_pair()
    subm.start_plane()

    wait_swapped(fsend, frecv, swap_sems.at[2], swap_sems.at[3], me, rep, False)
    child_cols = jnp.broadcast_to(child, (8, VOX)).T
    for group in range(groups):
        span = slice(group * group_rows, (group + 1) * group_rows)
        received = rows_of_group(frecv, group)
        kind = jnp.broadcast_to(child_cols[span, :1], (group_rows, L))
        for k in range(CHILDREN):
            cells_in[span, k * L:(k + 1) * L] = jnp.where(kind == k, received, 0.0).astype(BF)
    for quad in range(CHILDREN // 4):
        grads = dot(cgt[...], cells_in[:, quad * 4 * L:(quad + 1) * 4 * L])
        for i, packed in enumerate(pack(grads)):
            down.mine[(3 * quad + i) * C2:(3 * quad + i + 1) * C2] = packed
    down.mine[DOWN_TILES * C2:] = jnp.zeros((32 * DOWN_SHARE - DOWN_TILES * C2, L), F32)
    down.start_pair()
    subm.start_column()
    down.start_plane()

    def coarse_block(block):
        hits = onehot_of_row(cell - block * CHUNK, CHUNK)
        cells = dot(hits, cells_in[...]).astype(BF)
        coarse_ref[0, :, block * CHUNK:(block + 1) * CHUNK] = dot(cells, wdpad[...]).T[:C2].astype(BF)

    coarse_block(0)
    subm.start_back()
    down.start_column()
    coarse_block(1)
    subm.start_over()
    down.start_back()
    coarse_block(2)
    down.start_over()
    subm.finish()

    subm_ref[...] = subm.full[...]
    down.finish()
    dsum_ref[...] = down.full[...]
    wait_swapped(bsend, brecv, swap_sems.at[0], swap_sems.at[1], me, rep, True)
    wait_swapped(fsend, frecv, swap_sems.at[2], swap_sems.at[3], me, rep, True)
    subm.drain()
    down.drain()


def unpack_kernel(coarse_in, subm_ref, down_ref, coarse_ref, sgrad_ref, dgrad_ref):
    def unpack(full, rows, k):
        parts = [full[t * rows:(t + 1) * rows, lo:hi].astype(F32) for t, lo, hi in tiles_of_block(k)]
        parts.append(jnp.zeros((rows, L - C), F32))
        return jnp.concatenate(parts, axis=1)

    coarse_ref[...] = coarse_in[...]
    for k in range(OFFSETS):
        sgrad_ref[k] = padded_rows(unpack(subm_ref, C, k), L).T[:C, :C]
    for k in range(CHILDREN):
        dgrad_ref[k] = padded_rows(unpack(down_ref, C2, k), 2 * L).T[:C, :C2]


def per_device(
    voxel_feats, kernel_map, halo_down, halo_up, route_slot, recv_target,
    subm_weight, down_weight, coarse_grad,
):
    vmem = pl.BlockSpec(memory_space=pltpu.VMEM)
    swap = pltpu.VMEM((N_SPACE, PAD, L), BF)
    parts = pl.pallas_call(
        step_kernel,
        out_shape=(
            jax.ShapeDtypeStruct((1, C2, COARSE), BF),
            jax.ShapeDtypeStruct((32 * SUBM_SHARE, L), BF),
            jax.ShapeDtypeStruct((32 * DOWN_SHARE, L), BF),
        ),
        in_specs=[vmem] * 9,
        out_specs=(vmem,) * 3,
        scratch_shapes=[
            pltpu.VMEM((VOX, 2 * L), BF),
            pltpu.VMEM((VOX, L), BF),
            pltpu.VMEM((OWN_SUB, 2 * L), BF),
            pltpu.VMEM((RIM_SUB, 3 * L), BF),
            pltpu.VMEM((VOX, L), F32),
            pltpu.VMEM((OFFSETS * L, L), BF),
            pltpu.VMEM((CHILDREN * L, 2 * L), BF),
            pltpu.VMEM((VOX, QUADS * 4 * L), BF),
            pltpu.VMEM((VOX, L), F32),
            pltpu.VMEM((L, VOX), BF),
            pltpu.VMEM((C2, VOX), BF),
            pltpu.VMEM((VOX, L), F32),
            pltpu.VMEM((VOX, CHILDREN * L), BF),
            pltpu.VMEM((2, HALO, L), BF),
            pltpu.VMEM((2, HALO, L), BF),
            swap, swap, swap, swap,
            pltpu.SemaphoreType.DMA((2, 2)),
            pltpu.SemaphoreType.DMA((4,)),
            *Reducer.scratch(SUBM_SHARE),
            *Reducer.scratch(DOWN_SHARE),
        ],
        compiler_params=pltpu.CompilerParams(
            collective_id=0, has_side_effects=True, vmem_limit_bytes=56 * MIB
        ),
        name="step",
    )(
        voxel_feats, kernel_map.transpose(1, 0, 2), halo_up, halo_down, route_slot, recv_target,
        subm_weight, down_weight, coarse_grad,
    )
    return pl.pallas_call(
        unpack_kernel,
        out_shape=(
            jax.ShapeDtypeStruct((1, C2, COARSE), BF),
            jax.ShapeDtypeStruct((OFFSETS, C, C), F32),
            jax.ShapeDtypeStruct((CHILDREN, C, C2), F32),
        ),
        in_specs=[vmem] * 3,
        out_specs=(vmem,) * 3,
        name="unpack",
    )(*parts)


def solution(mesh):
    in_specs = (
        P("rep", None, "space"),
        P("rep", None, "space"),
        P("rep", "space"),
        P("rep", "space"),
        P("rep", "space"),
        P("rep", "space"),
        P(),
        P(),
        P("rep", None, "space"),
    )
    out_specs = (P("rep", None, "space"), P(), P())
    return jax.shard_map(
        per_device, mesh=mesh, in_specs=in_specs, out_specs=out_specs, check_vma=False
    )
```

```python
import jax
import jax.numpy as jnp
from jax import lax
from jax.experimental import pallas as pl
from jax.experimental.pallas import tpu as pltpu
from jax.sharding import PartitionSpec as P

C = 96
C2 = 192
OFFSETS = 27
CHILDREN = 8
VOX = 1536
HALO = 384
COARSE = 768
CAP = 24
N_SPACE = 64
N_REP = 4
L = 128
PAD = 32
OWN_SUB = 768
QUADS = 7
CHUNK = 256
STEP = 384
SEND_STEP = 192
EARLY = 1
PEERS_AT_ONCE = 8
MIB = 2**20
MESH = pl.DeviceIdType.MESH
BF = jnp.bfloat16
F32 = jnp.float32

SUBM_TILES = 21
DOWN_TILES = 6
SUBM_SHARE = 64
DOWN_SHARE = 48


def lane_iota(rows):
    return lax.broadcasted_iota(jnp.int32, (rows, L), 1).astype(F32).astype(BF)


def split_index(index):
    top = jnp.floor(index * (1.0 / L))
    return top.astype(BF), (index - L * top).astype(BF)


def onehot(top, low, iota, tiles):
    rows = iota.shape[0]
    zero = jnp.zeros((), BF)
    hit = jnp.where(jnp.broadcast_to(low, (rows, L)) == iota, jnp.ones((), BF), zero)
    tops = jnp.broadcast_to(top, (rows, L))
    return jnp.concatenate(
        [jnp.where(tops == jnp.asarray(t, BF), hit, zero) for t in range(tiles)], axis=1
    )


def onehot_of_row(row, rows):
    spread = jnp.broadcast_to(row, (rows, row.shape[1])).astype(BF)
    iota = lax.broadcasted_iota(jnp.int32, spread.shape, 0).astype(F32).astype(BF)
    return jnp.where(spread == iota, jnp.ones((), BF), jnp.zeros((), BF))


def padded_rows(x, rows):
    return jnp.concatenate([x, jnp.zeros((rows - x.shape[0], x.shape[1]), x.dtype)], axis=0)


def dot(a, b):
    return jnp.dot(a, b, preferred_element_type=F32)


def aligned(i, n):
    return pl.ds(pl.multiple_of(i * n, n), n)


def pack(blocks):
    piece = lambda k, lo, hi: blocks[:, k * L + lo:k * L + hi]
    return [
        jnp.concatenate([piece(0, 0, C), piece(1, 0, 32)], axis=1),
        jnp.concatenate([piece(1, 32, C), piece(2, 0, 64)], axis=1),
        jnp.concatenate([piece(2, 64, C), piece(3, 0, C)], axis=1),
    ]


def tiles_of_block(k):
    q, r = divmod(k, 4)
    pieces = []
    if r:
        pieces.append((3 * q + r - 1, L - 32 * r, L))
    if r < 3:
        pieces.append((3 * q + r, 0, C - 32 * r))
    return pieces


class Place:
    def __init__(self):
        space, y = lax.axis_index("space"), lax.axis_index("rep")
        core, z, x = space % 2, (space // 2) % 8, space // 16
        at = lambda xx, zz, cc: (xx * 8 + zz) * 2 + cc
        self.space, self.rep, self.core, self.z = space, y, core, z
        self.partner = (at(x, z, 1 - core), y)
        self.plane = [(at((x + d // 4) % 4, z, core), (y + d % 4) % 4) for d in range(16)]
        self.plane_to = [((x + d // 4) % 4) * 4 + (y + d % 4) % 4 for d in range(16)]
        self.plane_from = [((x + 4 - d // 4) % 4) * 4 + (y + 4 - d % 4) % 4 for d in range(16)]
        self.column = [(at(x, (z + d) % 8, core), y) for d in range(8)]
        self.column_from = [(z + 8 - d) % 8 for d in range(8)]


def remote(src, dst, sems, i, peer):
    return pltpu.make_async_remote_copy(
        src_ref=src, dst_ref=dst, send_sem=sems.at[0, i], recv_sem=sems.at[1, i],
        device_id=peer, device_id_type=MESH,
    )


class Reducer:
    @staticmethod
    def scratch(share):
        return [
            pltpu.VMEM((32 * share, L), F32),
            pltpu.VMEM((16 * share, L), BF),
            pltpu.VMEM((16 * share, L), BF),
            pltpu.VMEM((16, share, L), BF),
            pltpu.VMEM((16, share, L), BF),
            pltpu.VMEM((share, L), BF),
            pltpu.VMEM((8, share, L), BF),
            pltpu.VMEM((32 * share, L), BF),
            pltpu.SemaphoreType.DMA((2, 16)),
            pltpu.SemaphoreType.DMA((2, 16)),
            pltpu.SemaphoreType.DMA((2, 8)),
            pltpu.SemaphoreType.DMA((2, 16)),
            pltpu.SemaphoreType.DMA((2, 16)),
        ]

    def __init__(self, place, share, refs):
        self.place, self.share = place, share
        (self.mine, self.theirs, self.pair, self.psend, self.plane, self.zsend, self.column, self.full,
         self.pair_sems, self.plane_sems, self.z_sems, self.back_sems, self.over_sems) = refs
        self.sends = []

    def go(self, copy):
        copy.start()
        self.sends.append(copy)
        return copy

    def start_pair(self):
        p, n = self.place, self.share
        self.theirs[...] = self.mine[aligned(1 - p.core, 16 * n)].astype(BF)
        self.in_pair = []
        for d in range(16):
            at = aligned(p.plane_to[d], n)
            self.in_pair.append(self.go(
                remote(self.theirs.at[at], self.pair.at[at], self.pair_sems, d, p.partner)))

    def start_plane(self):
        p, n = self.place, self.share
        self.in_plane = []
        for d in list(range(1, 16)) + [0]:
            self.in_pair[d].wait_recv()
            both = (self.mine[aligned(p.core * 16 + p.plane_to[d], n)]
                    + self.pair[aligned(p.plane_to[d], n)].astype(F32))
            if d:
                self.psend[d] = both.astype(BF)
                self.in_plane.append(self.go(
                    remote(self.psend.at[d], self.plane.at[d], self.plane_sems, d, p.plane[d])))
        self.total = both

    def start_column(self):
        p = self.place
        total = self.total
        for d in range(1, 16):
            self.in_plane[d - 1].wait_recv()
            total += self.plane[d].astype(F32)
        self.zsend[...] = total.astype(BF)
        self.in_column = []
        for d in range(1, 8):
            self.in_column.append(self.go(
                remote(self.zsend, self.column.at[p.z], self.z_sems, d, p.column[d])))
        self.column[p.z] = total.astype(BF)

    def start_back(self):
        p, n = self.place, self.share
        for copy in self.in_column:
            copy.wait_recv()
        total = self.column[0].astype(F32)
        for z in range(1, 8):
            total += self.column[z].astype(F32)
        here = aligned(p.core * 16 + p.plane_to[0], n)
        self.full[here] = total.astype(BF)
        self.in_back = []
        for d in range(1, 16):
            self.in_back.append(self.go(
                remote(self.full.at[here], self.full.at[here], self.back_sems, d, p.plane[d])))

    def start_over(self):
        p, n = self.place, self.share
        self.in_over = []
        for d in range(16):
            if d:
                self.in_back[d - 1].wait_recv()
            at = aligned(p.core * 16 + p.plane_from[d], n)
            self.in_over.append(self.go(
                remote(self.full.at[at], self.full.at[at], self.over_sems, d, p.partner)))

    def finish(self):
        for copy in self.in_over:
            copy.wait_recv()

    def drain(self):
        for copy in self.sends:
            copy.wait_send()


def swap_copy(src, dst, send_sem, recv_sem, peer, me, rep):
    return pltpu.make_async_remote_copy(
        src_ref=src.at[peer], dst_ref=dst.at[me], send_sem=send_sem, recv_sem=recv_sem,
        device_id=(peer, rep), device_id_type=MESH,
    )


def wait_swapped(src, dst, send_sem, recv_sem, me, rep, sent):
    others = pl.ds(0, N_SPACE - 1)
    copies = pltpu.make_async_remote_copy(
        src_ref=src.at[others], dst_ref=dst.at[others], send_sem=send_sem, recv_sem=recv_sem,
        device_id=((me + 1) % N_SPACE, rep), device_id_type=MESH,
    )
    if sent:
        copies.wait_send()
    else:
        copies.wait_recv()


def rows_of_group(ref, group):
    return jnp.concatenate(
        [ref[group * PEERS_AT_ONCE + i].astype(F32)[:CAP] for i in range(PEERS_AT_ONCE)], axis=0
    )


def step_kernel(
    feats_ref, kmap_ref, up_ref, down_ref, route_ref, target_ref, w_ref, wd_ref, cg_ref,
    coarse_ref, subm_ref, dsum_ref,
    ordered, own, table, rim, which_buf, wpad, wdpad, gath, pre_buf, pre_grads, cgt, back, cells_in,
    hsend, hrecv, bsend, brecv, fsend, frecv, halo_sems, swap_sems, *reduce_refs,
):
    place = Place()
    me, rep = place.space, place.rep
    above, below = (me + 1) % N_SPACE, (me + N_SPACE - 1) % N_SPACE
    barrier = pltpu.get_barrier_semaphore()

    @pl.loop(1, N_SPACE)
    def _(d):
        pl.semaphore_signal(barrier, inc=1, device_id=((me + d) % N_SPACE, rep), device_id_type=MESH)

    others = [place.plane[d] for d in range(16) if d % 4]
    for peer in others:
        pl.semaphore_signal(barrier, inc=1, device_id=peer, device_id_type=MESH)

    own[...] = padded_rows(feats_ref[0].astype(F32), L).T.astype(BF)
    halo_rows = jnp.concatenate([up_ref[...], down_ref[...]], axis=1).astype(F32)
    halo_cols = jnp.broadcast_to(halo_rows, (8, 2 * HALO)).T
    iota_h = lane_iota(HALO)
    for side in range(2):
        top, low = split_index(halo_cols[side * HALO:(side + 1) * HALO, :1])
        hsend[side] = dot(onehot(top, low, iota_h, VOX // L), own[...]).astype(BF)

    target = target_ref[...].astype(F32)
    child = jnp.floor((target + 0.5) * (1.0 / COARSE))
    cell = target - COARSE * child
    wdpad[...] = jnp.zeros_like(wdpad)
    for k in range(CHILDREN):
        wdpad[k * L:k * L + C, :C2] = wd_ref[k]
    for block in range(VOX // CHUNK):
        span = slice(block * CHUNK, (block + 1) * CHUNK)
        hits = jnp.concatenate(
            [onehot_of_row(cell[:, span] - b * CHUNK, CHUNK) for b in range(COARSE // CHUNK)], axis=0
        )
        picked = dot(cg_ref[0], hits).astype(BF)
        cgt[:, span] = picked
        every = dot(wdpad[:, :C2], picked)
        chosen = jnp.zeros((L, CHUNK), F32)
        for k in range(CHILDREN):
            chosen = jnp.where(child[:, span] == k, every[k * L:(k + 1) * L], chosen)
        back[span, :] = chosen.T
    for peer in range(N_SPACE):
        bsend[peer] = padded_rows(back[peer * CAP:(peer + 1) * CAP], PAD).astype(BF)
    brecv[me] = bsend[me]

    neighbours = jnp.concatenate([kmap_ref[k] for k in range(OFFSETS)], axis=0).astype(F32)
    tile = jnp.floor(neighbours * (1.0 / L))
    parts = [padded_rows(x, PAD) for x in (tile, neighbours - L * tile)]
    ordered[:, :L] = padded_rows(jnp.concatenate(parts, axis=0), L).T.astype(BF)
    ordered[:, L:] = own[...]
    for j in range(2):
        table[:, j * L:(j + 1) * L] = own[j * OWN_SUB:(j + 1) * OWN_SUB]
    wpad[...] = jnp.zeros_like(wpad)
    for k in range(OFFSETS):
        wpad[k * L:k * L + C, :C] = w_ref[k]
    route = route_ref[...].astype(F32)
    iota_s = lane_iota(STEP)
    own_tiles = OWN_SUB // L

    def gather_own(turn):
        here = aligned(turn, STEP)
        start = (turn * STEP).astype(F32)
        hits = jnp.concatenate(
            [onehot_of_row(route - (start + off), STEP // 2) for off in (0.0, STEP / 2.0)], axis=0
        )
        mine = dot(hits, ordered[...])
        which = mine[:, :L]
        which_buf[here, :] = which
        pre_buf[here, :] = mine[:, L:]
        second = jnp.where(which >= own_tiles, 1.0, 0.0)
        top, low = (which - own_tiles * second).astype(BF), which.astype(BF)
        for k in range(OFFSETS):
            hot = onehot(top[:, k:k + 1], low[:, PAD + k:PAD + k + 1], iota_s, own_tiles)
            both = dot(hot, table[...])
            picked = jnp.where(second[:, k:k + 1] > 0.5, both[:, L:], both[:, :L])
            gath[here, k * L:(k + 1) * L] = picked.astype(BF)

    pl.loop(0, EARLY)(gather_own)

    to_upper = remote(hsend.at[0], hrecv.at[0], halo_sems, 0, (above, rep))
    to_lower = remote(hsend.at[1], hrecv.at[1], halo_sems, 1, (below, rep))
    pl.semaphore_wait(barrier, N_SPACE - 1 + len(others))
    to_upper.start()
    to_lower.start()

    @pl.loop(1, N_SPACE)
    def _(d):
        swap_copy(bsend, brecv, swap_sems.at[0], swap_sems.at[1], (me + d) % N_SPACE, me, rep).start()

    pl.loop(EARLY, VOX // STEP)(gather_own)

    to_upper.wait()
    to_lower.wait()
    rim[:, :L] = jnp.where(me > 0, hrecv[0], jnp.zeros((), BF))
    rim[:, L:] = jnp.where(me < N_SPACE - 1, hrecv[1], jnp.zeros((), BF))

    iota_r = lane_iota(SEND_STEP)
    peers = SEND_STEP // CAP
    rim_tiles = HALO // L

    @pl.loop(0, VOX // SEND_STEP)
    def _(i):
        turn = (me // peers + i) % (VOX // SEND_STEP)
        here = aligned(turn, SEND_STEP)
        which = which_buf[here, :]
        beyond = which - VOX // L
        kind = jnp.floor((beyond + 0.5) * (1.0 / rim_tiles))
        top, low = (beyond - rim_tiles * kind).astype(BF), which.astype(BF)
        for k in range(OFFSETS):
            lanes = slice(k * L, (k + 1) * L)
            hot = onehot(top[:, k:k + 1], low[:, PAD + k:PAD + k + 1], iota_r, rim_tiles)
            every = dot(hot, rim[...])
            kinds = jnp.broadcast_to(kind[:, k:k + 1], (SEND_STEP, L))
            picked = gath[here, lanes].astype(F32)
            for j in range(2):
                picked = jnp.where(kinds == j, every[:, j * L:(j + 1) * L], picked)
            gath[here, lanes] = picked.astype(BF)
        pre = pre_buf[here, :] + dot(gath[here, :OFFSETS * L], wpad[...])
        pre_buf[here, :] = pre
        fine = pre * jax.nn.sigmoid(pre)
        for j in range(peers):
            peer = turn * peers + j
            fsend[peer] = padded_rows(fine[j * CAP:(j + 1) * CAP], PAD).astype(BF)

            @pl.when(peer != me)
            def _():
                swap_copy(fsend, frecv, swap_sems.at[2], swap_sems.at[3], peer, me, rep).start()

    frecv[me] = fsend[me]

    half = len(reduce_refs) // 2
    subm = Reducer(place, SUBM_SHARE, reduce_refs[:half])
    down = Reducer(place, DOWN_SHARE, reduce_refs[half:])
    groups = N_SPACE // PEERS_AT_ONCE
    group_rows = PEERS_AT_ONCE * CAP
    wait_swapped(bsend, brecv, swap_sems.at[0], swap_sems.at[1], me, rep, False)
    for step in range(VOX // STEP):
        span = slice(step * STEP, (step + 1) * STEP)
        fine_grad = jnp.concatenate([rows_of_group(brecv, 2 * step + i) for i in range(2)], axis=0)
        pre = pre_buf[span, :]
        sig = jax.nn.sigmoid(pre)
        pre_grad = fine_grad * sig * (1.0 + pre * (1.0 - sig))
        pre_grads[:, span] = pre_grad.T.astype(BF)
    gath[:, OFFSETS * L:] = jnp.zeros((VOX, L), BF)
    for quad in range(QUADS):
        grads = dot(pre_grads[...], gath[:, quad * 4 * L:(quad + 1) * 4 * L])[:C]
        for i, packed in enumerate(pack(grads)):
            subm.mine[(3 * quad + i) * C:(3 * quad + i + 1) * C] = packed
    subm.mine[SUBM_TILES * C:] = jnp.zeros((32 * SUBM_SHARE - SUBM_TILES * C, L), F32)
    subm.start_pair()
    subm.start_plane()

    wait_swapped(fsend, frecv, swap_sems.at[2], swap_sems.at[3], me, rep, False)
    child_cols = jnp.broadcast_to(child, (8, VOX)).T
    for group in range(groups):
        span = slice(group * group_rows, (group + 1) * group_rows)
        received = rows_of_group(frecv, group)
        kind = jnp.broadcast_to(child_cols[span, :1], (group_rows, L))
        for k in range(CHILDREN):
            cells_in[span, k * L:(k + 1) * L] = jnp.where(kind == k, received, 0.0).astype(BF)
    for quad in range(CHILDREN // 4):
        grads = dot(cgt[...], cells_in[:, quad * 4 * L:(quad + 1) * 4 * L])
        for i, packed in enumerate(pack(grads)):
            down.mine[(3 * quad + i) * C2:(3 * quad + i + 1) * C2] = packed
    down.mine[DOWN_TILES * C2:] = jnp.zeros((32 * DOWN_SHARE - DOWN_TILES * C2, L), F32)
    down.start_pair()

    def coarse_block(block):
        hits = onehot_of_row(cell - block * CHUNK, CHUNK)
        cells = dot(hits, cells_in[...]).astype(BF)
        coarse_ref[0, :, block * CHUNK:(block + 1) * CHUNK] = dot(cells, wdpad[...]).T[:C2].astype(BF)

    coarse_block(0)
    subm.start_column()
    down.start_plane()
    coarse_block(1)
    subm.start_back()
    down.start_column()
    coarse_block(2)
    subm.start_over()
    down.start_back()
    down.start_over()
    subm.finish()

    subm_ref[...] = subm.full[...]
    down.finish()
    dsum_ref[...] = down.full[...]
    wait_swapped(bsend, brecv, swap_sems.at[0], swap_sems.at[1], me, rep, True)
    wait_swapped(fsend, frecv, swap_sems.at[2], swap_sems.at[3], me, rep, True)
    subm.drain()
    down.drain()


def unpack_kernel(coarse_in, subm_ref, down_ref, coarse_ref, sgrad_ref, dgrad_ref):
    def unpack(full, rows, k):
        parts = [full[t * rows:(t + 1) * rows, lo:hi].astype(F32) for t, lo, hi in tiles_of_block(k)]
        parts.append(jnp.zeros((rows, L - C), F32))
        return jnp.concatenate(parts, axis=1)

    coarse_ref[...] = coarse_in[...]
    for k in range(OFFSETS):
        sgrad_ref[k] = padded_rows(unpack(subm_ref, C, k), L).T[:C, :C]
    for k in range(CHILDREN):
        dgrad_ref[k] = padded_rows(unpack(down_ref, C2, k), 2 * L).T[:C, :C2]


def per_device(
    voxel_feats, kernel_map, halo_down, halo_up, route_slot, recv_target,
    subm_weight, down_weight, coarse_grad,
):
    vmem = pl.BlockSpec(memory_space=pltpu.VMEM)
    swap = pltpu.VMEM((N_SPACE, PAD, L), BF)
    parts = pl.pallas_call(
        step_kernel,
        out_shape=(
            jax.ShapeDtypeStruct((1, C2, COARSE), BF),
            jax.ShapeDtypeStruct((32 * SUBM_SHARE, L), BF),
            jax.ShapeDtypeStruct((32 * DOWN_SHARE, L), BF),
        ),
        in_specs=[vmem] * 9,
        out_specs=(vmem,) * 3,
        scratch_shapes=[
            pltpu.VMEM((VOX, 2 * L), BF),
            pltpu.VMEM((VOX, L), BF),
            pltpu.VMEM((OWN_SUB, 2 * L), BF),
            pltpu.VMEM((HALO, 2 * L), BF),
            pltpu.VMEM((VOX, L), F32),
            pltpu.VMEM((OFFSETS * L, L), BF),
            pltpu.VMEM((CHILDREN * L, 2 * L), BF),
            pltpu.VMEM((VOX, QUADS * 4 * L), BF),
            pltpu.VMEM((VOX, L), F32),
            pltpu.VMEM((L, VOX), BF),
            pltpu.VMEM((C2, VOX), BF),
            pltpu.VMEM((VOX, L), F32),
            pltpu.VMEM((VOX, CHILDREN * L), BF),
            pltpu.VMEM((2, HALO, L), BF),
            pltpu.VMEM((2, HALO, L), BF),
            swap, swap, swap, swap,
            pltpu.SemaphoreType.DMA((2, 2)),
            pltpu.SemaphoreType.DMA((4,)),
            *Reducer.scratch(SUBM_SHARE),
            *Reducer.scratch(DOWN_SHARE),
        ],
        compiler_params=pltpu.CompilerParams(
            collective_id=0, has_side_effects=True, vmem_limit_bytes=56 * MIB
        ),
        name="step",
    )(
        voxel_feats, kernel_map.transpose(1, 0, 2), halo_up, halo_down, route_slot, recv_target,
        subm_weight, down_weight, coarse_grad,
    )
    return pl.pallas_call(
        unpack_kernel,
        out_shape=(
            jax.ShapeDtypeStruct((1, C2, COARSE), BF),
            jax.ShapeDtypeStruct((OFFSETS, C, C), F32),
            jax.ShapeDtypeStruct((CHILDREN, C, C2), F32),
        ),
        in_specs=[vmem] * 3,
        out_specs=(vmem,) * 3,
        name="unpack",
    )(*parts)


def solution(mesh):
    in_specs = (
        P("rep", None, "space"),
        P("rep", None, "space"),
        P("rep", "space"),
        P("rep", "space"),
        P("rep", "space"),
        P("rep", "space"),
        P(),
        P(),
        P("rep", None, "space"),
    )
    out_specs = (P("rep", None, "space"), P(), P())
    return jax.shard_map(
        per_device, mesh=mesh, in_specs=in_specs, out_specs=out_specs, check_vma=False
    )
```

```python
import jax
import jax.numpy as jnp
from jax import lax
from jax.experimental import pallas as pl
from jax.experimental.pallas import tpu as pltpu
from jax.sharding import PartitionSpec as P

C = 96
C2 = 192
OFFSETS = 27
CHILDREN = 8
VOX = 1536
HALO = 384
COARSE = 768
CAP = 24
N_SPACE = 64
N_REP = 4
L = 128
PAD = 32
OWN_SUB = 768
QUADS = 7
CHUNK = 256
STEP = 384
SEND_STEP = 384
EARLY = 1
PEERS_AT_ONCE = 8
MIB = 2**20
MESH = pl.DeviceIdType.MESH
BF = jnp.bfloat16
F32 = jnp.float32

SUBM_TILES = 21
DOWN_TILES = 6
SUBM_SHARE = 64
DOWN_SHARE = 48


def lane_iota(rows):
    return lax.broadcasted_iota(jnp.int32, (rows, L), 1).astype(F32).astype(BF)


def split_index(index):
    top = jnp.floor(index * (1.0 / L))
    return top.astype(BF), (index - L * top).astype(BF)


def onehot(top, low, iota, tiles):
    rows = iota.shape[0]
    zero = jnp.zeros((), BF)
    hit = jnp.where(jnp.broadcast_to(low, (rows, L)) == iota, jnp.ones((), BF), zero)
    tops = jnp.broadcast_to(top, (rows, L))
    return jnp.concatenate(
        [jnp.where(tops == jnp.asarray(t, BF), hit, zero) for t in range(tiles)], axis=1
    )


def onehot_of_row(row, rows):
    spread = jnp.broadcast_to(row, (rows, row.shape[1])).astype(BF)
    iota = lax.broadcasted_iota(jnp.int32, spread.shape, 0).astype(F32).astype(BF)
    return jnp.where(spread == iota, jnp.ones((), BF), jnp.zeros((), BF))


def padded_rows(x, rows):
    return jnp.concatenate([x, jnp.zeros((rows - x.shape[0], x.shape[1]), x.dtype)], axis=0)


def dot(a, b):
    return jnp.dot(a, b, preferred_element_type=F32)


def aligned(i, n):
    return pl.ds(pl.multiple_of(i * n, n), n)


def pack(blocks):
    piece = lambda k, lo, hi: blocks[:, k * L + lo:k * L + hi]
    return [
        jnp.concatenate([piece(0, 0, C), piece(1, 0, 32)], axis=1),
        jnp.concatenate([piece(1, 32, C), piece(2, 0, 64)], axis=1),
        jnp.concatenate([piece(2, 64, C), piece(3, 0, C)], axis=1),
    ]


def tiles_of_block(k):
    q, r = divmod(k, 4)
    pieces = []
    if r:
        pieces.append((3 * q + r - 1, L - 32 * r, L))
    if r < 3:
        pieces.append((3 * q + r, 0, C - 32 * r))
    return pieces


class Place:
    def __init__(self):
        space, y = lax.axis_index("space"), lax.axis_index("rep")
        core, z, x = space % 2, (space // 2) % 8, space // 16
        at = lambda xx, zz, cc: (xx * 8 + zz) * 2 + cc
        self.space, self.rep, self.core, self.z = space, y, core, z
        self.partner = (at(x, z, 1 - core), y)
        self.plane = [(at((x + d // 4) % 4, z, core), (y + d % 4) % 4) for d in range(16)]
        self.plane_to = [((x + d // 4) % 4) * 4 + (y + d % 4) % 4 for d in range(16)]
        self.plane_from = [((x + 4 - d // 4) % 4) * 4 + (y + 4 - d % 4) % 4 for d in range(16)]
        self.column = [(at(x, (z + d) % 8, core), y) for d in range(8)]
        self.column_from = [(z + 8 - d) % 8 for d in range(8)]


def remote(src, dst, sems, i, peer):
    return pltpu.make_async_remote_copy(
        src_ref=src, dst_ref=dst, send_sem=sems.at[0, i], recv_sem=sems.at[1, i],
        device_id=peer, device_id_type=MESH,
    )


class Reducer:
    @staticmethod
    def scratch(share):
        return [
            pltpu.VMEM((32 * share, L), F32),
            pltpu.VMEM((16 * share, L), BF),
            pltpu.VMEM((16 * share, L), BF),
            pltpu.VMEM((16, share, L), BF),
            pltpu.VMEM((16, share, L), BF),
            pltpu.VMEM((share, L), BF),
            pltpu.VMEM((8, share, L), BF),
            pltpu.VMEM((32 * share, L), BF),
            pltpu.SemaphoreType.DMA((2, 16)),
            pltpu.SemaphoreType.DMA((2, 16)),
            pltpu.SemaphoreType.DMA((2, 8)),
            pltpu.SemaphoreType.DMA((2, 16)),
            pltpu.SemaphoreType.DMA((2, 16)),
        ]

    def __init__(self, place, share, refs):
        self.place, self.share = place, share
        (self.mine, self.theirs, self.pair, self.psend, self.plane, self.zsend, self.column, self.full,
         self.pair_sems, self.plane_sems, self.z_sems, self.back_sems, self.over_sems) = refs
        self.sends = []

    def go(self, copy):
        copy.start()
        self.sends.append(copy)
        return copy

    def start_pair(self):
        p, n = self.place, self.share
        self.theirs[...] = self.mine[aligned(1 - p.core, 16 * n)].astype(BF)
        self.in_pair = []
        for d in range(16):
            at = aligned(p.plane_to[d], n)
            self.in_pair.append(self.go(
                remote(self.theirs.at[at], self.pair.at[at], self.pair_sems, d, p.partner)))

    def start_plane(self):
        p, n = self.place, self.share
        self.in_plane = []
        for d in list(range(1, 16)) + [0]:
            self.in_pair[d].wait_recv()
            both = (self.mine[aligned(p.core * 16 + p.plane_to[d], n)]
                    + self.pair[aligned(p.plane_to[d], n)].astype(F32))
            if d:
                self.psend[d] = both.astype(BF)
                self.in_plane.append(self.go(
                    remote(self.psend.at[d], self.plane.at[d], self.plane_sems, d, p.plane[d])))
        self.total = both

    def start_column(self):
        p = self.place
        total = self.total
        for d in range(1, 16):
            self.in_plane[d - 1].wait_recv()
            total += self.plane[d].astype(F32)
        self.zsend[...] = total.astype(BF)
        self.in_column = []
        for d in range(1, 8):
            self.in_column.append(self.go(
                remote(self.zsend, self.column.at[p.z], self.z_sems, d, p.column[d])))
        self.column[p.z] = total.astype(BF)

    def start_back(self):
        p, n = self.place, self.share
        for copy in self.in_column:
            copy.wait_recv()
        total = self.column[0].astype(F32)
        for z in range(1, 8):
            total += self.column[z].astype(F32)
        here = aligned(p.core * 16 + p.plane_to[0], n)
        self.full[here] = total.astype(BF)
        self.in_back = []
        for d in range(1, 16):
            self.in_back.append(self.go(
                remote(self.full.at[here], self.full.at[here], self.back_sems, d, p.plane[d])))

    def start_over(self):
        p, n = self.place, self.share
        self.in_over = []
        for d in range(16):
            if d:
                self.in_back[d - 1].wait_recv()
            at = aligned(p.core * 16 + p.plane_from[d], n)
            self.in_over.append(self.go(
                remote(self.full.at[at], self.full.at[at], self.over_sems, d, p.partner)))

    def finish(self):
        for copy in self.in_over:
            copy.wait_recv()

    def drain(self):
        for copy in self.sends:
            copy.wait_send()


def swap_copy(src, dst, send_sem, recv_sem, peer, me, rep):
    return pltpu.make_async_remote_copy(
        src_ref=src.at[peer], dst_ref=dst.at[me], send_sem=send_sem, recv_sem=recv_sem,
        device_id=(peer, rep), device_id_type=MESH,
    )


def wait_swapped(src, dst, send_sem, recv_sem, me, rep, sent):
    others = pl.ds(0, N_SPACE - 1)
    copies = pltpu.make_async_remote_copy(
        src_ref=src.at[others], dst_ref=dst.at[others], send_sem=send_sem, recv_sem=recv_sem,
        device_id=((me + 1) % N_SPACE, rep), device_id_type=MESH,
    )
    if sent:
        copies.wait_send()
    else:
        copies.wait_recv()


def rows_of_group(ref, group):
    return jnp.concatenate(
        [ref[group * PEERS_AT_ONCE + i].astype(F32)[:CAP] for i in range(PEERS_AT_ONCE)], axis=0
    )


def step_kernel(
    feats_ref, kmap_ref, up_ref, down_ref, route_ref, target_ref, w_ref, wd_ref, cg_ref,
    coarse_ref, subm_ref, dsum_ref,
    ordered, own, table, rim, which_buf, wpad, wdpad, gath, pre_buf, pre_grads, cgt, back, cells_in,
    hsend, hrecv, bsend, brecv, fsend, frecv, halo_sems, swap_sems, *reduce_refs,
):
    place = Place()
    me, rep = place.space, place.rep
    above, below = (me + 1) % N_SPACE, (me + N_SPACE - 1) % N_SPACE
    barrier = pltpu.get_barrier_semaphore()

    @pl.loop(1, N_SPACE)
    def _(d):
        pl.semaphore_signal(barrier, inc=1, device_id=((me + d) % N_SPACE, rep), device_id_type=MESH)

    others = [place.plane[d] for d in range(16) if d % 4]
    for peer in others:
        pl.semaphore_signal(barrier, inc=1, device_id=peer, device_id_type=MESH)

    own[...] = padded_rows(feats_ref[0].astype(F32), L).T.astype(BF)
    halo_rows = jnp.concatenate([up_ref[...], down_ref[...]], axis=1).astype(F32)
    halo_cols = jnp.broadcast_to(halo_rows, (8, 2 * HALO)).T
    iota_h = lane_iota(HALO)
    for side in range(2):
        top, low = split_index(halo_cols[side * HALO:(side + 1) * HALO, :1])
        hsend[side] = dot(onehot(top, low, iota_h, VOX // L), own[...]).astype(BF)

    target = target_ref[...].astype(F32)
    child = jnp.floor((target + 0.5) * (1.0 / COARSE))
    cell = target - COARSE * child
    wdpad[...] = jnp.zeros_like(wdpad)
    for k in range(CHILDREN):
        wdpad[k * L:k * L + C, :C2] = wd_ref[k]
    for block in range(VOX // CHUNK):
        span = slice(block * CHUNK, (block + 1) * CHUNK)
        hits = jnp.concatenate(
            [onehot_of_row(cell[:, span] - b * CHUNK, CHUNK) for b in range(COARSE // CHUNK)], axis=0
        )
        picked = dot(cg_ref[0], hits).astype(BF)
        cgt[:, span] = picked
        every = dot(wdpad[:, :C2], picked)
        chosen = jnp.zeros((L, CHUNK), F32)
        for k in range(CHILDREN):
            chosen = jnp.where(child[:, span] == k, every[k * L:(k + 1) * L], chosen)
        back[span, :] = chosen.T
    for peer in range(N_SPACE):
        bsend[peer] = padded_rows(back[peer * CAP:(peer + 1) * CAP], PAD).astype(BF)
    brecv[me] = bsend[me]

    neighbours = jnp.concatenate([kmap_ref[k] for k in range(OFFSETS)], axis=0).astype(F32)
    tile = jnp.floor(neighbours * (1.0 / L))
    parts = [padded_rows(x, PAD) for x in (tile, neighbours - L * tile)]
    ordered[:, :L] = padded_rows(jnp.concatenate(parts, axis=0), L).T.astype(BF)
    ordered[:, L:] = own[...]
    for j in range(2):
        table[:, j * L:(j + 1) * L] = own[j * OWN_SUB:(j + 1) * OWN_SUB]
    wpad[...] = jnp.zeros_like(wpad)
    for k in range(OFFSETS):
        wpad[k * L:k * L + C, :C] = w_ref[k]
    route = route_ref[...].astype(F32)
    iota_s = lane_iota(STEP)
    own_tiles = OWN_SUB // L

    def gather_own(turn):
        here = aligned(turn, STEP)
        start = (turn * STEP).astype(F32)
        hits = jnp.concatenate(
            [onehot_of_row(route - (start + off), STEP // 2) for off in (0.0, STEP / 2.0)], axis=0
        )
        mine = dot(hits, ordered[...])
        which = mine[:, :L]
        which_buf[here, :] = which
        pre_buf[here, :] = mine[:, L:]
        second = jnp.where(which >= own_tiles, 1.0, 0.0)
        top, low = (which - own_tiles * second).astype(BF), which.astype(BF)
        for k in range(OFFSETS):
            hot = onehot(top[:, k:k + 1], low[:, PAD + k:PAD + k + 1], iota_s, own_tiles)
            both = dot(hot, table[...])
            picked = jnp.where(second[:, k:k + 1] > 0.5, both[:, L:], both[:, :L])
            gath[here, k * L:(k + 1) * L] = picked.astype(BF)

    pl.loop(0, EARLY)(gather_own)

    to_upper = remote(hsend.at[0], hrecv.at[0], halo_sems, 0, (above, rep))
    to_lower = remote(hsend.at[1], hrecv.at[1], halo_sems, 1, (below, rep))
    pl.semaphore_wait(barrier, N_SPACE - 1 + len(others))
    to_upper.start()
    to_lower.start()

    @pl.loop(1, N_SPACE)
    def _(d):
        swap_copy(bsend, brecv, swap_sems.at[0], swap_sems.at[1], (me + d) % N_SPACE, me, rep).start()

    pl.loop(EARLY, VOX // STEP)(gather_own)

    to_upper.wait()
    to_lower.wait()
    rim[:, :L] = jnp.where(me > 0, hrecv[0], jnp.zeros((), BF))
    rim[:, L:] = jnp.where(me < N_SPACE - 1, hrecv[1], jnp.zeros((), BF))

    iota_r = lane_iota(SEND_STEP)
    peers = SEND_STEP // CAP
    rim_tiles = HALO // L

    @pl.loop(0, VOX // SEND_STEP)
    def _(i):
        turn = (me // peers + i) % (VOX // SEND_STEP)
        here = aligned(turn, SEND_STEP)
        which = which_buf[here, :]
        beyond = which - VOX // L
        kind = jnp.floor((beyond + 0.5) * (1.0 / rim_tiles))
        top, low = (beyond - rim_tiles * kind).astype(BF), which.astype(BF)
        for k in range(OFFSETS):
            lanes = slice(k * L, (k + 1) * L)
            hot = onehot(top[:, k:k + 1], low[:, PAD + k:PAD + k + 1], iota_r, rim_tiles)
            every = dot(hot, rim[...])
            kinds = jnp.broadcast_to(kind[:, k:k + 1], (SEND_STEP, L))
            picked = gath[here, lanes].astype(F32)
            for j in range(2):
                picked = jnp.where(kinds == j, every[:, j * L:(j + 1) * L], picked)
            gath[here, lanes] = picked.astype(BF)
        pre = pre_buf[here, :] + dot(gath[here, :OFFSETS * L], wpad[...])
        pre_buf[here, :] = pre
        fine = pre * jax.nn.sigmoid(pre)
        for j in range(peers):
            peer = turn * peers + j
            fsend[peer] = padded_rows(fine[j * CAP:(j + 1) * CAP], PAD).astype(BF)

            @pl.when(peer != me)
            def _():
                swap_copy(fsend, frecv, swap_sems.at[2], swap_sems.at[3], peer, me, rep).start()

    frecv[me] = fsend[me]

    half = len(reduce_refs) // 2
    subm = Reducer(place, SUBM_SHARE, reduce_refs[:half])
    down = Reducer(place, DOWN_SHARE, reduce_refs[half:])
    groups = N_SPACE // PEERS_AT_ONCE
    group_rows = PEERS_AT_ONCE * CAP
    wait_swapped(bsend, brecv, swap_sems.at[0], swap_sems.at[1], me, rep, False)
    for step in range(VOX // STEP):
        span = slice(step * STEP, (step + 1) * STEP)
        fine_grad = jnp.concatenate([rows_of_group(brecv, 2 * step + i) for i in range(2)], axis=0)
        pre = pre_buf[span, :]
        sig = jax.nn.sigmoid(pre)
        pre_grad = fine_grad * sig * (1.0 + pre * (1.0 - sig))
        pre_grads[:, span] = pre_grad.T.astype(BF)
    gath[:, OFFSETS * L:] = jnp.zeros((VOX, L), BF)
    for quad in range(QUADS):
        grads = dot(pre_grads[...], gath[:, quad * 4 * L:(quad + 1) * 4 * L])[:C]
        for i, packed in enumerate(pack(grads)):
            subm.mine[(3 * quad + i) * C:(3 * quad + i + 1) * C] = packed
    subm.mine[SUBM_TILES * C:] = jnp.zeros((32 * SUBM_SHARE - SUBM_TILES * C, L), F32)
    subm.start_pair()
    subm.start_plane()

    wait_swapped(fsend, frecv, swap_sems.at[2], swap_sems.at[3], me, rep, False)
    child_cols = jnp.broadcast_to(child, (8, VOX)).T
    for group in range(groups):
        span = slice(group * group_rows, (group + 1) * group_rows)
        received = rows_of_group(frecv, group)
        kind = jnp.broadcast_to(child_cols[span, :1], (group_rows, L))
        for k in range(CHILDREN):
            cells_in[span, k * L:(k + 1) * L] = jnp.where(kind == k, received, 0.0).astype(BF)
    for quad in range(CHILDREN // 4):
        grads = dot(cgt[...], cells_in[:, quad * 4 * L:(quad + 1) * 4 * L])
        for i, packed in enumerate(pack(grads)):
            down.mine[(3 * quad + i) * C2:(3 * quad + i + 1) * C2] = packed
    down.mine[DOWN_TILES * C2:] = jnp.zeros((32 * DOWN_SHARE - DOWN_TILES * C2, L), F32)
    down.start_pair()

    def coarse_block(block):
        hits = onehot_of_row(cell - block * CHUNK, CHUNK)
        cells = dot(hits, cells_in[...]).astype(BF)
        coarse_ref[0, :, block * CHUNK:(block + 1) * CHUNK] = dot(cells, wdpad[...]).T[:C2].astype(BF)

    coarse_block(0)
    subm.start_column()
    down.start_plane()
    coarse_block(1)
    subm.start_back()
    down.start_column()
    coarse_block(2)
    subm.start_over()
    down.start_back()
    down.start_over()
    subm.finish()

    subm_ref[...] = subm.full[...]
    down.finish()
    dsum_ref[...] = down.full[...]
    wait_swapped(bsend, brecv, swap_sems.at[0], swap_sems.at[1], me, rep, True)
    wait_swapped(fsend, frecv, swap_sems.at[2], swap_sems.at[3], me, rep, True)
    subm.drain()
    down.drain()


def unpack_kernel(coarse_in, subm_ref, down_ref, coarse_ref, sgrad_ref, dgrad_ref):
    def unpack(full, rows, k):
        parts = [full[t * rows:(t + 1) * rows, lo:hi].astype(F32) for t, lo, hi in tiles_of_block(k)]
        parts.append(jnp.zeros((rows, L - C), F32))
        return jnp.concatenate(parts, axis=1)

    coarse_ref[...] = coarse_in[...]
    for k in range(OFFSETS):
        sgrad_ref[k] = padded_rows(unpack(subm_ref, C, k), L).T[:C, :C]
    for k in range(CHILDREN):
        dgrad_ref[k] = padded_rows(unpack(down_ref, C2, k), 2 * L).T[:C, :C2]


def per_device(
    voxel_feats, kernel_map, halo_down, halo_up, route_slot, recv_target,
    subm_weight, down_weight, coarse_grad,
):
    vmem = pl.BlockSpec(memory_space=pltpu.VMEM)
    swap = pltpu.VMEM((N_SPACE, PAD, L), BF)
    parts = pl.pallas_call(
        step_kernel,
        out_shape=(
            jax.ShapeDtypeStruct((1, C2, COARSE), BF),
            jax.ShapeDtypeStruct((32 * SUBM_SHARE, L), BF),
            jax.ShapeDtypeStruct((32 * DOWN_SHARE, L), BF),
        ),
        in_specs=[vmem] * 9,
        out_specs=(vmem,) * 3,
        scratch_shapes=[
            pltpu.VMEM((VOX, 2 * L), BF),
            pltpu.VMEM((VOX, L), BF),
            pltpu.VMEM((OWN_SUB, 2 * L), BF),
            pltpu.VMEM((HALO, 2 * L), BF),
            pltpu.VMEM((VOX, L), F32),
            pltpu.VMEM((OFFSETS * L, L), BF),
            pltpu.VMEM((CHILDREN * L, 2 * L), BF),
            pltpu.VMEM((VOX, QUADS * 4 * L), BF),
            pltpu.VMEM((VOX, L), F32),
            pltpu.VMEM((L, VOX), BF),
            pltpu.VMEM((C2, VOX), BF),
            pltpu.VMEM((VOX, L), F32),
            pltpu.VMEM((VOX, CHILDREN * L), BF),
            pltpu.VMEM((2, HALO, L), BF),
            pltpu.VMEM((2, HALO, L), BF),
            swap, swap, swap, swap,
            pltpu.SemaphoreType.DMA((2, 2)),
            pltpu.SemaphoreType.DMA((4,)),
            *Reducer.scratch(SUBM_SHARE),
            *Reducer.scratch(DOWN_SHARE),
        ],
        compiler_params=pltpu.CompilerParams(
            collective_id=0, has_side_effects=True, vmem_limit_bytes=56 * MIB
        ),
        name="step",
    )(
        voxel_feats, kernel_map.transpose(1, 0, 2), halo_up, halo_down, route_slot, recv_target,
        subm_weight, down_weight, coarse_grad,
    )
    return pl.pallas_call(
        unpack_kernel,
        out_shape=(
            jax.ShapeDtypeStruct((1, C2, COARSE), BF),
            jax.ShapeDtypeStruct((OFFSETS, C, C), F32),
            jax.ShapeDtypeStruct((CHILDREN, C, C2), F32),
        ),
        in_specs=[vmem] * 3,
        out_specs=(vmem,) * 3,
        name="unpack",
    )(*parts)


def solution(mesh):
    in_specs = (
        P("rep", None, "space"),
        P("rep", None, "space"),
        P("rep", "space"),
        P("rep", "space"),
        P("rep", "space"),
        P("rep", "space"),
        P(),
        P(),
        P("rep", None, "space"),
    )
    out_specs = (P("rep", None, "space"), P(), P())
    return jax.shard_map(
        per_device, mesh=mesh, in_specs=in_specs, out_specs=out_specs, check_vma=False
    )
```
